256 devices in a mesh: dp: 32 (over x, z), ctx: 8 (over y, core).
Axes of the slice: x: 4, y: 4, z: 8, core: 2. Of those that a mesh axis runs over, the one named last changes fastest.
Arguments:
- normed_input: bfloat16 [32, 1024, 5120], P('dp', 'ctx'), may hold values from -6 to 6
- queries: bfloat16 [32, 1024, 8192], P('dp', 'ctx'), may hold values from -150 to 150
- keys: bfloat16 [32, 1024, 1024], P('dp', 'ctx'), may hold values from -6 to 6
- values: bfloat16 [32, 1024, 1024], P('dp', 'ctx'), may hold values from -6 to 6
- out_grad: bfloat16 [32, 1024, 8192], P('dp', 'ctx'), may hold values from -6 to 6
- loss_weight: int32 [32, 1024], P('dp', 'ctx'), may hold values from 0 to 3
- doc_ids: int32 [32, 1024], P('dp', 'ctx'), may hold values from 0 to 3, never falling along the last dimension, each value on 1 to 512 neighbouring positions
- adapter: float32 [64, 19456], P(None, 'dp'), may hold values from -0.078125 to 0.078125
- moment1: float32 [64, 19456], P(None, 'dp'), may hold values from -4 to 4
- moment2: float32 [64, 19456], P(None, 'dp'), may hold values from 0.05 to 1
Outputs:
- new_moment1: float32 [64, 19456], P(None, 'dp')
- new_moment2: float32 [64, 19456], P(None, 'dp')
- adam_step: float32 [64, 19456], P(None, 'dp')
The draws below stay inside these ranges and needn't reach their ends.
Inputs may be any that keep to these rules, and one draw needn't show every extreme that they name: `doc_ids`: within a sequence document ids never fall; each document is whole and one has exactly 512 positions.
All inputs are finite; a program needn't handle non-finite values.
Results may differ from the reference program's by a relative error of at most 0.0094.
Values may be sent and summed in bfloat16 or wider, within the bound.
A program may use at most 128 MiB of HBM per device.

```python
import math
import jax
import jax.numpy as jnp
import numpy as np
from jax import lax

D = 5120
QUERY_HEADS = 64
KEY_VALUE_HEADS = 8
HEAD_SIZE = 128
RANK = 64
ROLLOUT_LENGTH = 1024
PACKED_SEQUENCES = 32
FACT = 19456
N_DP = 32


def base_keys(key):
    return jax.random.truncated_normal(key, -6.0, 6.0, (PACKED_SEQUENCES, ROLLOUT_LENGTH, KEY_VALUE_HEADS * HEAD_SIZE), jnp.float32)


def draw_keys(key, part):
    frozen_weight = base_keys(key)
    return frozen_weight.astype(jnp.bfloat16)


def draw_queries(key, part):
    key = jax.random.fold_in(key, 23)
    own = jax.random.truncated_normal(key, -6.0, 6.0, (PACKED_SEQUENCES, ROLLOUT_LENGTH, QUERY_HEADS * HEAD_SIZE), jnp.float32)
    return own.astype(jnp.bfloat16)


def place_ends(values, key, smallest, high):
    index_at = [jax.random.randint(jax.random.fold_in(key, axis), (), 0, length) for axis, length in enumerate(values.shape)]
    widest = values.shape.index(max(values.shape))
    neighbour = index_at[:widest] + [(index_at[widest] + 1) % values.shape[widest]] + index_at[widest + 1:]
    return values.at[tuple(index_at)].set(smallest).at[tuple(neighbour)].set(high)


def block_levels(own_key, extent, cuts, least, largest):
    def one(position, blocks):
        draws = jax.random.uniform(jax.random.fold_in(jax.random.fold_in(own_key, 6), position), (blocks,), jnp.float32, least / len(cuts), largest / len(cuts))
        return jnp.repeat(jnp.exp(draws), extent[position] // blocks).reshape((-1,) + (1,) * (len(extent) - position - 1))

    gain = one(*cuts[0])
    for cut in cuts[1:]:
        gain = gain * one(*cut)
    return gain


def split_up(number_of, total, limit, skew):
    portions = [(1 << 20) // math.isqrt(standing ** skew) + 1 for standing in range(2, number_of + 1)]
    rest, holding = total - limit - (number_of - 1), [1] * (number_of - 1)
    while rest > 0:
        movable = [i for i in range(number_of - 1) if holding[i] < limit]
        whole, remaining = sum([portions[i] for i in movable]), rest
        for i in movable:
            extra = min(limit - holding[i], max(1, remaining * portions[i] // whole), rest)
            holding[i] = holding[i] + extra
            rest = rest - extra
    return np.array([limit] + holding)


def uneven(own_key, count, total, limit, lean):
    if count == 2:
        one = jax.random.randint(own_key, (), max(1, total - limit), min(limit, total - 1) + 1)
        return jnp.stack([one, total - one])
    tallies = jnp.asarray(split_up(count, total, limit, lean), jnp.int32)
    couples = (count - 1) // 2
    giver, sink = tallies[1:1 + 2 * couples:2], tallies[2:2 + 2 * couples:2]
    room = jnp.minimum(giver - 1, limit - sink)
    moved = jax.random.randint(jax.random.fold_in(own_key, 1), (couples,), 0, 1 << 20) % (room + 1)
    tallies = tallies.at[1:1 + 2 * couples:2].set(giver - moved).at[2:2 + 2 * couples:2].set(sink + moved)
    return tallies[jax.random.permutation(jax.random.fold_in(own_key, 2), count)]


def bell_draw(key, shape, spread, limit, shards=(), held_as=jnp.bfloat16):
    level = block_levels(key, shape, shards, -0.22, 0.18) if shards else 1.0
    result = jax.random.normal(key, shape, jnp.float32) * spread * level
    return jnp.minimum(jnp.maximum(result, -limit), limit).astype(held_as)


def setup_inputs(seed: int = 0) -> dict:
    arg_keys = jax.random.split(jax.random.key(seed), 11)
    return {
        "normed_input": bell_draw(arg_keys[0], (PACKED_SEQUENCES, ROLLOUT_LENGTH, D), 1.0, 6.0, ((0, 32), (1, 8))),
        "queries": draw_queries(jax.random.fold_in(arg_keys[10], 71), 0),
        "keys": draw_keys(jax.random.fold_in(arg_keys[10], 71), 0),
        "values": bell_draw(arg_keys[3], (PACKED_SEQUENCES, ROLLOUT_LENGTH, KEY_VALUE_HEADS * HEAD_SIZE), 1.0, 6.0, ((0, 32), (1, 8))),
        "out_grad": bell_draw(arg_keys[4], (PACKED_SEQUENCES, ROLLOUT_LENGTH, QUERY_HEADS * HEAD_SIZE), 1.0, 6.0, ((0, 32), (1, 8))),
        "loss_weight": place_ends(jax.random.randint(arg_keys[5], (PACKED_SEQUENCES, ROLLOUT_LENGTH), 0, 4), jax.random.fold_in(arg_keys[5], 1), 0, 3).astype(jnp.int32),
        "doc_ids": jax.vmap(lambda own: jnp.searchsorted(jnp.cumsum(uneven(own, 4, ROLLOUT_LENGTH, ROLLOUT_LENGTH // 2, 0)), jnp.arange(ROLLOUT_LENGTH), side="right"))(jax.random.split(arg_keys[6], PACKED_SEQUENCES)).reshape((PACKED_SEQUENCES, ROLLOUT_LENGTH)).astype(jnp.int32),
        "adapter": bell_draw(arg_keys[7], (RANK, FACT), D ** -0.5, 0.078125, ((1, 32),), jnp.float32),
        "moment1": bell_draw(arg_keys[8], (RANK, FACT), 0.3, 4.0, ((1, 32),), jnp.float32),
        "moment2": jnp.clip(jnp.exp(math.log(1.0) - 2.9957323 * jax.random.uniform(arg_keys[9], (RANK, FACT), jnp.float32) ** block_levels(arg_keys[9], (RANK, FACT), ((1, 32),), -0.2, 0.2)), 0.05, 1.0),
    }


THETA = 1000000.0
ADAPTER_SCALE = 2.0
BETA_ONE = 0.9
BETA_TWO = 0.95
ADAM_EPS = 1e-08
STEP_COUNT = 10

def head_backward(query_h, key_g, value_g, cot_h, docs):
    sequence_length, width = query_h.shape
    block = min(sequence_length, 512)
    scale = 1.0 / width ** 0.5
    key_pos = jnp.arange(sequence_length, dtype=jnp.int32)

    def one_block(acc, index):
        start = (index * block).astype(jnp.int32)
        q_rows = lax.dynamic_slice_in_dim(query_h, start, block, 0)
        g_rows = lax.dynamic_slice_in_dim(cot_h, start, block, 0)
        d_rows = lax.dynamic_slice_in_dim(docs, start, block, 0)
        q_pos = start + jnp.arange(block, dtype=jnp.int32)
        scores = lax.dot_general(q_rows, key_g, (((1,), (1,)), ((), ())), preferred_element_type=jnp.float32) * scale
        allowed = (key_pos[None, :] <= q_pos[:, None]) & (docs[None, :] == d_rows[:, None])
        scores = jnp.where(allowed, scores, -jnp.inf)
        top = lax.optimization_barrier(jnp.max(scores, axis=1, keepdims=True))
        expo = jnp.exp(scores - top)
        probs = expo / lax.optimization_barrier(jnp.sum(expo, axis=1, keepdims=True))
        probs_b = probs.astype(jnp.bfloat16)
        dprobs = lax.dot_general(g_rows, value_g, (((1,), (1,)), ((), ())), preferred_element_type=jnp.float32)
        delta = lax.optimization_barrier(jnp.sum(probs * dprobs, axis=1, keepdims=True))
        dscores = (probs * (dprobs - delta) * scale).astype(jnp.bfloat16)
        dq_rows = jnp.dot(dscores, key_g, preferred_element_type=jnp.float32).astype(jnp.bfloat16)
        acc = acc + lax.dot_general(probs_b, g_rows, (((0,), (0,)), ((), ())), preferred_element_type=jnp.float32)
        return (acc, dq_rows)
    dv_acc, dq_blocks = lax.scan(one_block, jnp.zeros((sequence_length, width), jnp.float32), jnp.arange(sequence_length // block, dtype=jnp.int32))
    return (dq_blocks.reshape(sequence_length, width), dv_acc)

def group_backward(query_g, key_g, value_g, cot_g, docs):
    sequence_length, head_w = key_g.shape
    group = query_g.shape[1] // head_w
    q_heads = query_g.reshape(sequence_length, group, head_w).transpose(1, 0, 2)
    c_heads = cot_g.reshape(sequence_length, group, head_w).transpose(1, 0, 2)

    def one_head(acc, pair):
        dq_h, dv_h = head_backward(pair[0], key_g, value_g, pair[1], docs)
        return (acc + dv_h, dq_h)
    dv_sum, dq_heads = lax.scan(one_head, jnp.zeros((sequence_length, head_w), jnp.float32), (q_heads, c_heads))
    return (dq_heads.transpose(1, 0, 2).reshape(sequence_length, group * head_w), dv_sum.astype(jnp.bfloat16))

def rope_back(dq_rot, start, head_w):
    sequence_length, width = dq_rot.shape
    half = head_w // 2
    pos = start.astype(jnp.float32) + jnp.arange(sequence_length, dtype=jnp.float32)
    freq = THETA ** (-(jnp.arange(half, dtype=jnp.float32) * 2.0 / head_w))
    angle = pos[:, None] * freq[None, :]
    cosine = jnp.cos(angle)[:, None, :]
    sine = jnp.sin(angle)[:, None, :]
    upper = dq_rot.astype(jnp.float32).reshape(sequence_length, width // head_w, head_w)
    first = upper[:, :, :half]
    second = upper[:, :, half:]
    out_first = first * cosine + second * sine
    out_second = second * cosine - first * sine
    return jnp.concatenate([out_first, out_second], axis=2).reshape(sequence_length, width).astype(jnp.bfloat16)

def adapter_gradient(hidden_rows, query_gradient, dv, lowrank_factors):
    width = hidden_rows.shape[1]
    q_width = query_gradient.shape[1]
    a_query = lowrank_factors[:, :width]
    a_value = lowrank_factors[:, width:2 * width]
    b_query = lowrank_factors[:, 2 * width:2 * width + q_width]
    b_value = lowrank_factors[:, 2 * width + q_width:]
    inner = (((1,), (1,)), ((), ()))
    outer = (((0,), (0,)), ((), ()))
    low_q = lax.dot_general(hidden_rows, a_query, inner, preferred_element_type=jnp.float32).astype(jnp.bfloat16)
    low_v = lax.dot_general(hidden_rows, a_value, inner, preferred_element_type=jnp.float32).astype(jnp.bfloat16)
    mid_q = lax.dot_general(query_gradient, b_query, inner, preferred_element_type=jnp.float32).astype(jnp.bfloat16)
    mid_v = lax.dot_general(dv, b_value, inner, preferred_element_type=jnp.float32).astype(jnp.bfloat16)
    grad_aq = lax.dot_general(mid_q, hidden_rows, outer, preferred_element_type=jnp.float32)
    grad_av = lax.dot_general(mid_v, hidden_rows, outer, preferred_element_type=jnp.float32)
    grad_bq = lax.dot_general(low_q, query_gradient, outer, preferred_element_type=jnp.float32)
    grad_bv = lax.dot_general(low_v, dv, outer, preferred_element_type=jnp.float32)
    return jnp.concatenate([grad_aq, grad_av, grad_bq, grad_bv], axis=1)

def adam_update(gradient_tree, moment1, moment2):
    new_m = BETA_ONE * moment1 + (1.0 - BETA_ONE) * gradient_tree
    new_v = BETA_TWO * moment2 + (1.0 - BETA_TWO) * gradient_tree * gradient_tree
    corr_one = 1.0 - BETA_ONE ** STEP_COUNT
    corr_two = 1.0 - BETA_TWO ** STEP_COUNT
    step = new_m / corr_one / (jnp.sqrt(new_v / corr_two) + ADAM_EPS)
    return (new_m, new_v, step)

def reference(normed_input, queries, keys, values, out_grad, loss_weight, doc_ids, adapter, moment1, moment2):
    lowrank_factors = adapter.astype(jnp.bfloat16)
    sequence_length = queries.shape[1]

    def one_sequence(acc, items):
        x_seq, query_sequence, key_sequence, value_sequence, g_seq, w_seq, d_seq = items
        weighted_values = (g_seq * w_seq[:, None].astype(jnp.float32)).astype(jnp.bfloat16)
        query_groups = query_sequence.reshape(sequence_length, KEY_VALUE_HEADS, -1).transpose(1, 0, 2)
        gradient_groups = weighted_values.reshape(sequence_length, KEY_VALUE_HEADS, -1).transpose(1, 0, 2)
        key_groups = key_sequence.reshape(sequence_length, KEY_VALUE_HEADS, HEAD_SIZE).transpose(1, 0, 2)
        value_groups = value_sequence.reshape(sequence_length, KEY_VALUE_HEADS, HEAD_SIZE).transpose(1, 0, 2)
        dq_g, dv_g = lax.map(lambda grp: group_backward(grp[0], grp[1], grp[2], grp[3], d_seq), (query_groups, key_groups, value_groups, gradient_groups))
        dq_rot = dq_g.transpose(1, 0, 2).reshape(sequence_length, -1)
        dv = dv_g.transpose(1, 0, 2).reshape(sequence_length, -1)
        query_gradient = rope_back(dq_rot, jnp.zeros((), jnp.int32), HEAD_SIZE)
        return (acc + adapter_gradient(x_seq, query_gradient, dv, lowrank_factors), None)
    total_sum, unused = lax.scan(one_sequence, jnp.zeros(adapter.shape, jnp.float32), (normed_input, queries, keys, values, out_grad, loss_weight, doc_ids))
    gradient_tree = total_sum * (ADAPTER_SCALE / N_DP)
    return adam_update(gradient_tree, moment1, moment2)
```

```python
import functools

import jax
import jax.numpy as jnp
import numpy as np
from jax import lax
from jax.experimental import pallas as pl
from jax.experimental.pallas import tpu as pltpu
from jax.sharding import PartitionSpec as P

HEAD = 128
GROUP = 8
KV = 8
D = 5120
RANK = 64
ROWS = 128
BLOCKS = 5
WINDOW = BLOCKS * ROWS
QW = KV * GROUP * HEAD
FACT = 2 * D + QW + KV * HEAD
BQ = 2 * D
BV = BQ + QW
NX, NZ, NY, NC = 4, 8, 4, 2
SHARD = FACT // (NX * NZ)
XCOLS = FACT // NX
HALF = XCOLS // 2
CUT = 1152
REST = HALF - CUT
WIN = 768

THETA = 1000000.0
ADAPTER_SCALE = 2.0
BETA_ONE = 0.9
BETA_TWO = 0.95
ADAM_EPS = 1e-08
STEP_COUNT = 10
NEG = -1e30
MESH = pl.DeviceIdType.MESH
NT = (((1,), (1,)), ((), ()))
NN = (((1,), (0,)), ((), ()))
F32 = jnp.float32
BF16 = jnp.bfloat16


def rope_tables():
    freq = THETA ** (-(np.arange(HEAD // 2, dtype=np.float64) * 2.0 / HEAD))
    angle = freq[:, None] * np.arange(NY * NC * ROWS, dtype=np.float64)[None, :]
    both = np.stack([np.cos(angle), np.sin(angle)])
    return both.reshape(2, HEAD // 2, NY * NC, ROWS).transpose(2, 0, 1, 3).astype(np.float32)


def dot(a, b, dims):
    return lax.dot_general(a, b, dims, preferred_element_type=F32)


def attention_kernel(
    q_ref, g_ref, lw_ref, docs_ref, k_ref, v_ref, table_ref,
    dq_ref, dv_ref,
    kv_buf, doc_buf, bias, lw_t, table, p_buf, w_buf, kt_buf,
    table_sem, doc_send, doc_recv, send_sem, recv_sem,
):
    dp = lax.axis_index("dp")
    c = lax.axis_index("ctx")
    y = c // 2
    core = c % 2

    table_copy = pltpu.make_async_copy(table_ref.at[c], table, table_sem)
    table_copy.start()

    barrier = pltpu.get_barrier_semaphore()
    for j in range(1, BLOCKS):
        @pl.when(c >= j)
        def _():
            pl.semaphore_signal(barrier, inc=1, device_id=(dp, c - j), device_id_type=MESH)

        @pl.when(c + j < 8)
        def _():
            pl.semaphore_signal(barrier, inc=1, device_id=(dp, c + j), device_id_type=MESH)

    own = BLOCKS - 1
    doc_buf[own] = jnp.broadcast_to(docs_ref[...].astype(F32), (8, ROWS))
    for h in range(KV):
        kv_buf[h, own, 0] = k_ref[:, h * HEAD:(h + 1) * HEAD]
        kv_buf[h, own, 1] = v_ref[:, h * HEAD:(h + 1) * HEAD]

    for slot in range(own):
        @pl.when(c + slot < own)
        def _():
            doc_buf[slot] = jnp.full((8, ROWS), -1.0, F32)
            for h in range(KV):
                kv_buf[h, slot] = jnp.zeros((2, ROWS, HEAD), BF16)

    pl.semaphore_wait(barrier, jnp.minimum(c, own) + jnp.minimum(7 - c, own))

    def doc_copy(j):
        return pltpu.make_async_remote_copy(
            src_ref=doc_buf.at[own], dst_ref=doc_buf.at[own - j],
            send_sem=doc_send.at[j - 1], recv_sem=doc_recv.at[own - j],
            device_id=(dp, c + j), device_id_type=MESH)

    def kv_copy(h, kind, source, target, peer):
        return pltpu.make_async_remote_copy(
            src_ref=kv_buf.at[h, source], dst_ref=kv_buf.at[h, target],
            send_sem=send_sem.at[h, kind], recv_sem=recv_sem.at[h, target],
            device_id=(dp, peer), device_id_type=MESH)

    def hop_own(h):
        return kv_copy(h, 0, 4, 2, c + 2)

    def pair_own(h):
        return kv_copy(h, 1, 4, 3, c + 1)

    def hop_relay(h):
        return kv_copy(h, 2, 2, 0, c + 2)

    def pair_near_up(h):
        return kv_copy(h, 3, 2, 1, c + 1)

    def pair_near_down(h):
        return kv_copy(h, 3, 2, 3, c - 1)

    def pair_far_down(h):
        return kv_copy(h, 4, 0, 1, c - 1)

    for j in range(1, BLOCKS):
        @pl.when(c + j < 8)
        def _():
            doc_copy(j).start()

    def send_own(h, carry):
        @pl.when(y < 3)
        def _():
            hop_own(h).start()

        @pl.when(core == 0)
        def _():
            pair_own(h).start()
        return carry

    lax.fori_loop(0, KV, send_own, 0)

    def relay_near(h):
        @pl.when(y >= 1)
        def _():
            hop_own(h).wait_recv()

            @pl.when(y < 3)
            def _():
                hop_relay(h).start()

            @pl.when(core == 0)
            def _():
                pair_near_up(h).start()

            @pl.when(core == 1)
            def _():
                pair_near_down(h).start()

    def relay_far(h):
        @pl.when(y >= 2)
        def _():
            hop_relay(h).wait_recv()

            @pl.when(core == 1)
            def _():
                pair_far_down(h).start()

    def arrive(h):
        @pl.when(jnp.logical_or(core == 1, y >= 1))
        def _():
            pair_own(h).wait_recv()

        @pl.when(jnp.logical_or(y >= 2, jnp.logical_and(core == 1, y >= 1)))
        def _():
            pair_far_down(h).wait_recv()

    lw_t[...] = jnp.broadcast_to(lw_ref[...].astype(F32), (ROWS, ROWS)).T
    table_copy.wait()
    relay_near(0)
    relay_near(1)
    for slot in range(own):
        @pl.when(c + slot >= own)
        def _():
            doc_copy(own - slot).wait_recv()
    doc_row = doc_buf[own][0:1, :]
    row_pos = lax.broadcasted_iota(jnp.int32, (ROWS, ROWS), 1)
    key_pos = lax.broadcasted_iota(jnp.int32, (ROWS, ROWS), 0)
    for slot in range(BLOCKS):
        doc_col = jnp.broadcast_to(doc_buf[slot][0:1, :], (ROWS, ROWS)).T
        allowed = doc_col == doc_row
        if slot == own:
            allowed = jnp.logical_and(allowed, key_pos <= row_pos)
        block = jnp.where(allowed, 0.0, NEG)
        bias[slot * ROWS:(slot + 1) * ROWS, 0:ROWS] = block
        bias[slot * ROWS:(slot + 1) * ROWS, ROWS:] = block
    relay_far(0)

    scale = 1.0 / HEAD ** 0.5
    fold = scale * float(np.log2(np.e))

    def one_group(h, carry):
        @pl.when(h + 2 < KV)
        def _():
            relay_near(h + 2)

        @pl.when(h + 1 < KV)
        def _():
            relay_far(h + 1)

        arrive(h)
        keys = kv_buf[h, :, 0].reshape(WINDOW, HEAD)
        vals = kv_buf[h, :, 1].reshape(WINDOW, HEAD)
        kt_buf[...] = keys.astype(F32).T.astype(BF16)
        cosine = jnp.concatenate([table[0], table[0]], axis=1)
        sine = jnp.concatenate([table[1], table[1]], axis=1)
        for pair in range(GROUP // 2):
            cols = [
                pl.ds(pl.multiple_of(h * GROUP * HEAD + (2 * pair + t) * HEAD, HEAD), HEAD)
                for t in range(2)
            ]
            q_two = jnp.concatenate([q_ref[:, cols[0]], q_ref[:, cols[1]]], axis=0)
            w_two = jnp.concatenate(
                [(g_ref[:, s].astype(F32) * lw_t[...]).astype(BF16) for s in cols], axis=0)
            w_buf[pair * 256:(pair + 1) * 256, :] = w_two
            scores = dot(keys, q_two, NT) + bias[...]
            top = jnp.max(scores, axis=0, keepdims=True)
            expo = jnp.exp2((scores - top) * fold)
            probs = expo * (1.0 / jnp.sum(expo, axis=0, keepdims=True))
            dprobs = dot(vals, w_two, NT)
            delta = jnp.sum(probs * dprobs, axis=0, keepdims=True)
            p_buf[:, pair * 256:(pair + 1) * 256] = probs.astype(BF16)
            dscores = (probs * (dprobs - delta)).astype(BF16)
            dq = dot(kt_buf[...], dscores, NN) * scale
            dq = dq.astype(BF16).astype(F32)
            first, second = dq[0:64], dq[64:128]
            out = jnp.concatenate(
                [first * cosine + second * sine, second * cosine - first * sine], axis=0
            ).astype(BF16)
            base = h * GROUP * HEAD + 2 * pair * HEAD
            dq_ref[pl.ds(pl.multiple_of(base, HEAD), HEAD), :] = out[:, 0:ROWS]
            dq_ref[pl.ds(pl.multiple_of(base + HEAD, HEAD), HEAD), :] = out[:, ROWS:]
        dv = dot(p_buf[...], w_buf[...], NN)
        dv_ref[:, pl.ds(pl.multiple_of(h * HEAD, HEAD), HEAD)] = dv.astype(BF16)
        return carry

    lax.fori_loop(0, KV, one_group, 0)

    for j in range(1, BLOCKS):
        @pl.when(c + j < 8)
        def _():
            doc_copy(j).wait_send()

    def drain(h, carry):
        @pl.when(y < 3)
        def _():
            hop_own(h).wait_send()

        @pl.when(core == 0)
        def _():
            pair_own(h).wait_send()

        @pl.when(y >= 1)
        def _():
            pair_near_up(h).wait_send()

            @pl.when(y < 3)
            def _():
                hop_relay(h).wait_send()

        @pl.when(jnp.logical_and(y >= 2, core == 1))
        def _():
            pair_far_down(h).wait_send()
        return carry

    lax.fori_loop(0, KV, drain, 0)


def attention(q, g, lw, docs, k, v):
    vmem = pl.BlockSpec(memory_space=pltpu.VMEM)
    return pl.pallas_call(
        attention_kernel,
        out_shape=(
            jax.ShapeDtypeStruct((QW, ROWS), BF16),
            jax.ShapeDtypeStruct((WINDOW, KV * HEAD), BF16),
        ),
        in_specs=[vmem] * 6 + [pl.BlockSpec(memory_space=pl.ANY)],
        out_specs=(vmem, vmem),
        scratch_shapes=[
            pltpu.VMEM((KV, BLOCKS, 2, ROWS, HEAD), BF16),
            pltpu.VMEM((BLOCKS, 8, ROWS), F32),
            pltpu.VMEM((WINDOW, 2 * ROWS), F32),
            pltpu.VMEM((ROWS, ROWS), F32),
            pltpu.VMEM((2, HEAD // 2, ROWS), F32),
            pltpu.VMEM((WINDOW, GROUP * ROWS), BF16),
            pltpu.VMEM((GROUP * ROWS, HEAD), BF16),
            pltpu.VMEM((HEAD, WINDOW), BF16),
            pltpu.SemaphoreType.DMA,
            pltpu.SemaphoreType.DMA((BLOCKS - 1,)),
            pltpu.SemaphoreType.DMA((BLOCKS - 1,)),
            pltpu.SemaphoreType.DMA((KV, 5)),
            pltpu.SemaphoreType.DMA((KV, BLOCKS - 1)),
        ],
        compiler_params=pltpu.CompilerParams(
            collective_id=0, has_side_effects=True, vmem_limit_bytes=48 * 1024 * 1024),
        cost_estimate=pl.CostEstimate(
            flops=8 * 64 * WINDOW * ROWS * HEAD, bytes_accessed=10_000_000,
            transcendentals=64 * WINDOW * ROWS),
        name="attention_back",
    )(q, g, lw, docs, k, v, jnp.asarray(rope_tables()))


def reduce_kernel(
    dq_ref, dv_ref, x_ref, f_ref, m1_ref, m2_ref,
    o1_ref, o2_ref, o3_ref,
    grad, low_buf, mid_part, mid_buf, core_buf, stage, ry, rx, s2a, s2b, ry2, rx2,
    total, z_out, rz, z_sum, full,
    low_send, low_recv, mid_send, mid_recv, core_send, core_recv,
    y_send, y_recv, x_send, x_recv, x2_send, x2_recv, y2_send, y2_recv,
    z_send, z_recv, f_send, f_recv,
):
    dp = lax.axis_index("dp")
    c = lax.axis_index("ctx")
    x, z = dp // NZ, dp % NZ
    y, core = c // 2, c % 2
    own = BLOCKS - 1

    def at(xx, zz, yy, cc):
        return (xx * NZ + zz, yy * 2 + cc)

    def ahead(value, step, size):
        return (value + step) % size

    def push(src, dst, send, recv, peer):
        return pltpu.make_async_remote_copy(
            src_ref=src, dst_ref=dst, send_sem=send, recv_sem=recv,
            device_id=peer, device_id_type=MESH)

    barrier = pltpu.get_barrier_semaphore()
    peers = [(dp, ahead(c, j, 8)) for j in range(1, 8)]
    peers += [at(ahead(x, d, NX), z, y, core) for d in range(1, NX)]
    peers += [at(x, ahead(z, d, NZ), y, core) for d in range(1, NZ)]
    for peer in peers:
        pl.semaphore_signal(barrier, inc=1, device_id=peer, device_id_type=MESH)

    low_q = dot(f_ref[:, 0:D], x_ref[...], NT).astype(BF16)
    low_v = dot(f_ref[:, D:2 * D], x_ref[...], NT).astype(BF16)
    low_buf[own] = low_v
    for slot in range(own):
        @pl.when(c + slot < own)
        def _():
            low_buf[slot] = jnp.zeros((RANK, ROWS), BF16)

        @pl.when(c + slot + 1 > 7)
        def _():
            mid_buf[slot] = jnp.zeros((RANK, ROWS), F32)

    part = dot(f_ref[:, BV:FACT], dv_ref[...], NT)
    for slot in range(BLOCKS):
        mid_part[slot] = part[:, slot * ROWS:(slot + 1) * ROWS]

    pl.semaphore_wait(barrier, len(peers))

    def low_copy(j):
        return push(low_buf.at[own], low_buf.at[own - j], low_send.at[j - 1],
                    low_recv.at[own - j], (dp, c + j))

    def mid_copy(j):
        return push(mid_part.at[own - j], mid_buf.at[j - 1], mid_send.at[j - 1],
                    mid_recv.at[j - 1], (dp, c - j))

    for j in range(1, BLOCKS):
        @pl.when(c + j < 8)
        def _():
            low_copy(j).start()

        @pl.when(c >= j)
        def _():
            mid_copy(j).start()

    mid_q = dot(f_ref[:, BQ:BV], dq_ref[...], NN).astype(BF16)
    for i in range(KV):
        grad[:, BQ + i * 1024:BQ + (i + 1) * 1024] = dot(
            low_q, dq_ref[i * 1024:(i + 1) * 1024, :], NT)
    for slot in range(own):
        @pl.when(c + slot >= own)
        def _():
            low_copy(own - slot).wait_recv()
    low_window = jnp.concatenate([low_buf[s] for s in range(BLOCKS)], axis=1)
    grad[:, BV:FACT] = dot(low_window, dv_ref[...], NN)

    def core_copy(part_x):
        return push(
            grad.at[:, pl.ds(pl.multiple_of(part_x * XCOLS + (1 - core) * HALF, HEAD), HALF)],
            core_buf.at[part_x], core_send.at[part_x], core_recv.at[part_x],
            at(x, z, y, 1 - core))

    core_copy(3).start()
    for i in range(5):
        cols = slice(i * 1024, (i + 1) * 1024)
        grad[:, cols] = dot(mid_q, x_ref[:, cols], NN)
    core_copy(0).start()
    mid_v = mid_part[own]
    for j in range(1, BLOCKS):
        @pl.when(c + j < 8)
        def _():
            mid_copy(j).wait_recv()
        mid_v = mid_v + mid_buf[j - 1]
    mid_v = mid_v.astype(BF16)
    for i in range(5):
        grad[:, D + i * 1024:D + (i + 1) * 1024] = dot(
            mid_v, x_ref[:, i * 1024:(i + 1) * 1024], NN)
    core_copy(1).start()
    core_copy(2).start()

    def y_rows(yy):
        return pl.ds(pl.multiple_of(yy * 16, 16), 16)

    def y_copy(d, part_x):
        yy = ahead(y, d, NY)
        return push(stage.at[part_x, y_rows(yy), 0:CUT], ry.at[d - 1, part_x],
                    y_send.at[d - 1, part_x], y_recv.at[d - 1, part_x], at(x, z, yy, core))

    def x_copy(d):
        xx = ahead(x, d, NX)
        return push(stage.at[xx, :, CUT:HALF], rx.at[d - 1],
                    x_send.at[d - 1], x_recv.at[d - 1], at(xx, z, y, core))

    for part_x in (3, 0, 1, 2):
        core_copy(part_x).wait_recv()
        mine = grad[:, pl.ds(pl.multiple_of(part_x * XCOLS + core * HALF, HEAD), HALF)]
        stage[part_x] = (mine + core_buf[part_x]).astype(BF16)
        for d in range(1, NY):
            y_copy(d, part_x).start()
        for d in range(1, NX):
            @pl.when(ahead(x, d, NX) == part_x)
            def _():
                x_copy(d).start()

    def x2_copy(d):
        return push(s2a.at[d - 1], rx2.at[d - 1], x2_send.at[d - 1], x2_recv.at[d - 1],
                    at(ahead(x, d, NX), z, y, core))

    def y2_copy(d):
        return push(s2b.at[d - 1], ry2.at[d - 1], y2_send.at[d - 1], y2_recv.at[d - 1],
                    at(x, z, ahead(y, d, NY), core))

    for part_x in (3, 0, 1, 2):
        for d in range(1, NY):
            y_copy(d, part_x).wait_recv()
    for d in (1, 2, 3, 0):
        xx = ahead(x, d, NX)
        value = stage[xx, y_rows(y), 0:CUT].astype(F32)
        for e in range(NY - 1):
            value = value + ry[e, xx].astype(F32)
        if d:
            s2a[d - 1] = value.astype(BF16)
            x2_copy(d).start()
        else:
            total[:, 0:CUT] = value
    for d in range(1, NX):
        x_copy(d).wait_recv()
    for d in (1, 2, 3, 0):
        yy = ahead(y, d, NY)
        value = stage[x, y_rows(yy), CUT:HALF].astype(F32)
        for e in range(NX - 1):
            value = value + rx[e, y_rows(yy), :].astype(F32)
        if d:
            s2b[d - 1] = value.astype(BF16)
            y2_copy(d).start()
        else:
            total[:, CUT:HALF] = value
    for d in range(1, NX):
        x2_copy(d).wait_recv()
    value = total[:, 0:CUT]
    for e in range(NX - 1):
        value = value + rx2[e].astype(F32)
    total[:, 0:CUT] = value
    for d in range(1, NY):
        y2_copy(d).wait_recv()
    value = total[:, CUT:HALF]
    for e in range(NY - 1):
        value = value + ry2[e].astype(F32)
    total[:, CUT:HALF] = value
    z_out[...] = total[...].astype(BF16)

    starts = (0, 512, 1152, 1664)

    def z_copy(quarter, slot):
        return push(z_out.at[:, starts[quarter]:starts[quarter] + WIN], rz.at[slot],
                    z_send.at[quarter], z_recv.at[slot], at(x, core * 4 + quarter, y, core))

    for quarter in range(4):
        @pl.when(core * 4 + quarter != z)
        def _():
            z_copy(quarter, z).start()

    def full_copy(j):
        return push(full.at[y_rows(y)], full.at[y_rows(y)], f_send.at[j - 1],
                    f_recv.at[y], (dp, ahead(c, j, 8)))

    holder = z // 4

    @pl.when(core == holder)
    def _():
        for quarter in range(4):
            @pl.when(z % 4 == quarter)
            def _():
                z_sum[...] = total[:, starts[quarter]:starts[quarter] + WIN]
        value = z_sum[...]
        for s in range(1, NZ):
            slot = ahead(z, s, NZ)
            z_copy(0, slot).wait_recv()
            value = value + rz[slot].astype(F32)
        for quarter in range(4):
            @pl.when(z % 4 == quarter)
            def _():
                shift = quarter * SHARD - starts[quarter]
                moved = pltpu.roll(value, WIN - shift, axis=1) if shift else value
                full[y_rows(y), :] = moved[:, 0:640]
        for j in range(1, 8):
            full_copy(j).start()

    def row_wait(yy):
        pltpu.make_async_remote_copy(
            src_ref=full.at[y_rows(yy)], dst_ref=full.at[y_rows(yy)], send_sem=f_send.at[0],
            recv_sem=f_recv.at[yy], device_id=(dp, ahead(c, 1, 8)),
            device_id_type=MESH).wait_recv()

    for d in range(1, NY):
        row_wait(ahead(y, d, NY))

    @pl.when(core != holder)
    def _():
        row_wait(y)

    gradient = full[:, 0:SHARD] * (ADAPTER_SCALE / (NX * NZ))
    new_m = BETA_ONE * m1_ref[...] + (1.0 - BETA_ONE) * gradient
    new_v = BETA_TWO * m2_ref[...] + (1.0 - BETA_TWO) * gradient * gradient
    corr_one = 1.0 - BETA_ONE ** STEP_COUNT
    corr_two = 1.0 - BETA_TWO ** STEP_COUNT
    o1_ref[...] = new_m
    o2_ref[...] = new_v
    o3_ref[...] = new_m / corr_one / (jnp.sqrt(new_v / corr_two) + ADAM_EPS)

    for j in range(1, BLOCKS):
        @pl.when(c + j < 8)
        def _():
            low_copy(j).wait_send()

        @pl.when(c >= j)
        def _():
            mid_copy(j).wait_send()
    for part_x in range(NX):
        core_copy(part_x).wait_send()
        for d in range(1, NY):
            y_copy(d, part_x).wait_send()
    for d in range(1, NX):
        x_copy(d).wait_send()
        x2_copy(d).wait_send()
        y2_copy(d).wait_send()
    for quarter in range(4):
        @pl.when(core * 4 + quarter != z)
        def _():
            z_copy(quarter, z).wait_send()

    @pl.when(core == holder)
    def _():
        for j in range(1, 8):
            full_copy(j).wait_send()


def reduce_and_step(dq, dv, x, factors, m1, m2):
    vmem = pl.BlockSpec(memory_space=pltpu.VMEM)
    dma = pltpu.SemaphoreType.DMA
    out = jax.ShapeDtypeStruct((RANK, SHARD), F32)
    return pl.pallas_call(
        reduce_kernel,
        out_shape=(out, out, out),
        in_specs=[vmem] * 6,
        out_specs=(vmem, vmem, vmem),
        scratch_shapes=[
            pltpu.VMEM((RANK, FACT), F32),
            pltpu.VMEM((BLOCKS, RANK, ROWS), BF16),
            pltpu.VMEM((BLOCKS, RANK, ROWS), F32),
            pltpu.VMEM((BLOCKS - 1, RANK, ROWS), F32),
            pltpu.VMEM((NX, RANK, HALF), F32),
            pltpu.VMEM((NX, RANK, HALF), BF16),
            pltpu.VMEM((NY - 1, NX, 16, CUT), BF16),
            pltpu.VMEM((NX - 1, RANK, REST), BF16),
            pltpu.VMEM((NX - 1, 16, CUT), BF16),
            pltpu.VMEM((NY - 1, 16, REST), BF16),
            pltpu.VMEM((NY - 1, 16, REST), BF16),
            pltpu.VMEM((NX - 1, 16, CUT), BF16),
            pltpu.VMEM((16, HALF), F32),
            pltpu.VMEM((16, HALF), BF16),
            pltpu.VMEM((NZ, 16, WIN), BF16),
            pltpu.VMEM((16, WIN), F32),
            pltpu.VMEM((RANK, 640), F32),
            dma((4,)), dma((4,)), dma((4,)), dma((4,)), dma((4,)), dma((4,)),
            dma((3, 4)), dma((3, 4)), dma((3,)), dma((3,)),
            dma((3,)), dma((3,)), dma((3,)), dma((3,)),
            dma((4,)), dma((8,)), dma((7,)), dma((4,)),
        ],
        compiler_params=pltpu.CompilerParams(
            collective_id=1, has_side_effects=True, vmem_limit_bytes=48 * 1024 * 1024),
        cost_estimate=pl.CostEstimate(
            flops=4 * FACT * RANK * ROWS, bytes_accessed=10_000_000, transcendentals=0),
        name="reduce_and_step",
    )(dq, dv, x, factors, m1, m2)


def per_device(
    normed_input, queries, keys, values, out_grad, loss_weight, doc_ids, adapter, moment1, moment2
):
    factors = lax.all_gather(adapter.astype(BF16), "dp", axis=1, tiled=True)
    dq, dv = attention(
        queries[0], out_grad[0], loss_weight, doc_ids, keys[0], values[0])
    return reduce_and_step(dq, dv, normed_input[0], factors, moment1, moment2)


def solution(mesh):
    in_specs = (
        P("dp", "ctx", None),
        P("dp", "ctx", None),
        P("dp", "ctx", None),
        P("dp", "ctx", None),
        P("dp", "ctx", None),
        P("dp", "ctx"),
        P("dp", "ctx"),
        P(None, "dp"),
        P(None, "dp"),
        P(None, "dp"),
    )
    out_specs = (P(None, "dp"), P(None, "dp"), P(None, "dp"))
    return jax.shard_map(
        per_device, mesh=mesh, in_specs=in_specs, out_specs=out_specs, check_vma=False
    )
```

```python
import functools

import jax
import jax.numpy as jnp
import numpy as np
from jax import lax
from jax.experimental import pallas as pl
from jax.experimental.pallas import tpu as pltpu
from jax.sharding import PartitionSpec as P

HEAD = 128
GROUP = 8
KV = 8
D = 5120
RANK = 64
ROWS = 128
BLOCKS = 5
WINDOW = BLOCKS * ROWS
QW = KV * GROUP * HEAD
FACT = 2 * D + QW + KV * HEAD
BQ = 2 * D
BV = BQ + QW
NX, NZ, NY, NC = 4, 8, 4, 2
SHARD = FACT // (NX * NZ)
XCOLS = FACT // NX
HALF = XCOLS // 2
HALF_ROWS = RANK // 2
CUT = 1152
REST = HALF - CUT
WIN = 768

THETA = 1000000.0
ADAPTER_SCALE = 2.0
BETA_ONE = 0.9
BETA_TWO = 0.95
ADAM_EPS = 1e-08
STEP_COUNT = 10
NEG = -1e30
MESH = pl.DeviceIdType.MESH
NT = (((1,), (1,)), ((), ()))
NN = (((1,), (0,)), ((), ()))
F32 = jnp.float32
BF16 = jnp.bfloat16


def rope_tables():
    freq = THETA ** (-(np.arange(HEAD // 2, dtype=np.float64) * 2.0 / HEAD))
    angle = np.arange(NY * NC * ROWS, dtype=np.float64)[:, None] * freq[None, :]
    cosine, sine = np.cos(angle), np.sin(angle)
    both = np.stack(
        [np.concatenate([cosine, cosine], axis=1), np.concatenate([sine, -sine], axis=1)])
    return both.reshape(2, NY * NC, ROWS, HEAD).transpose(1, 0, 2, 3).astype(np.float32)


def dot(a, b, dims):
    return lax.dot_general(a, b, dims, preferred_element_type=F32)


def turn(a):
    return a.astype(F32).T.astype(BF16)


def kernel(
    q_hbm, g_hbm, lw_hbm, docs_hbm, k_hbm, v_hbm, x_hbm, a_hbm, table_hbm,
    out_ref,
    q_ref, g_ref, lw_ref, docs_ref, x_ref, a_ref, table,
    kv_buf, back_buf, doc_buf, bias, lw_t, w_buf, dq_ref, dv_ref,
    a_roll, z_in, f_ref,
    grad, low_buf, mid_part, mid_buf, core_buf, stage, ry, rx, s2a, s2b, ry2, rx2,
    total, z_out, rz, z_sum, full,
    in_sem, q_sem, g_sem, kv_sem, doc_send, doc_recv, send_sem, recv_sem, back_recv,
    fz_send, fz_recv, fx_send, fx_recv, fc_send, fc_recv,
    low_send, low_recv, mid_send, mid_recv, core_send, core_recv,
    y_send, y_recv, x_send, x_recv, x2_send, x2_recv, y2_send, y2_recv,
    z_send, z_recv, f_send, f_recv,
):
    dp = lax.axis_index("dp")
    c = lax.axis_index("ctx")
    x, z = dp // NZ, dp % NZ
    y, core = c // 2, c % 2
    own = BLOCKS - 1

    def at(xx, zz, yy, cc):
        return (xx * NZ + zz, yy * 2 + cc)

    def ahead(value, step, size):
        return (value + step) % size

    def push(src, dst, send, recv, peer):
        return pltpu.make_async_remote_copy(
            src_ref=src, dst_ref=dst, send_sem=send, recv_sem=recv,
            device_id=peer, device_id_type=MESH)

    def cols_of(h, width):
        return pl.ds(pl.multiple_of(h * width, width), width)

    def kv_load(h, which):
        source = k_hbm if which == 0 else v_hbm
        return pltpu.make_async_copy(
            source.at[:, cols_of(h, HEAD)], kv_buf.at[h, own, which], kv_sem.at[h, which])

    def q_load(h):
        return pltpu.make_async_copy(
            q_hbm.at[:, cols_of(h, 1024)], q_ref.at[:, cols_of(h, 1024)], q_sem.at[h])

    def g_load(h):
        return pltpu.make_async_copy(
            g_hbm.at[:, cols_of(h, 1024)], g_ref.at[:, cols_of(h, 1024)], g_sem.at[h])

    small = [
        pltpu.make_async_copy(docs_hbm, docs_ref, in_sem.at[0]),
        pltpu.make_async_copy(a_hbm, a_ref, in_sem.at[1]),
        pltpu.make_async_copy(lw_hbm, lw_ref, in_sem.at[2]),
        pltpu.make_async_copy(table_hbm.at[c], table, in_sem.at[3]),
        pltpu.make_async_copy(x_hbm, x_ref, in_sem.at[4]),
    ]
    barrier = pltpu.get_barrier_semaphore()
    peers = [(dp, ahead(c, j, 8)) for j in range(1, 8)]
    peers += [at(ahead(x, d, NX), z, y, core) for d in range(1, NX)]
    peers += [at(x, ahead(z, d, NZ), y, core) for d in range(1, NZ)]
    for peer in peers:
        pl.semaphore_signal(barrier, inc=1, device_id=peer, device_id_type=MESH)
    small[0].start()
    small[1].start()

    def load_kv(h, carry):
        kv_load(h, 0).start()
        kv_load(h, 1).start()
        return carry

    lax.fori_loop(0, KV, load_kv, 0)
    small[2].start()
    small[3].start()

    def load_qg(h, carry):
        q_load(h).start()
        g_load(h).start()
        return carry

    lax.fori_loop(0, KV, load_qg, 0)
    small[4].start()

    for slot in range(own):
        @pl.when(c + slot < own)
        def _():
            doc_buf[slot] = jnp.full((8, ROWS), -1.0, F32)
            low_buf[slot] = jnp.zeros((RANK, ROWS), BF16)
            for h in range(KV):
                kv_buf[h, slot] = jnp.zeros((2, ROWS, HEAD), BF16)

        @pl.when(c + slot + 1 > 7)
        def _():
            mid_buf[slot] = jnp.zeros((RANK, ROWS), F32)

    small[0].wait()
    doc_buf[own] = jnp.broadcast_to(docs_ref[...].astype(F32), (8, ROWS))
    pl.semaphore_wait(barrier, len(peers))

    def doc_copy(j):
        return push(doc_buf.at[own], doc_buf.at[own - j], doc_send.at[j - 1],
                    doc_recv.at[own - j], (dp, c + j))

    def kv_copy(h, kind, source, target, peer):
        return push(kv_buf.at[h, source], kv_buf.at[h, target], send_sem.at[h, kind],
                    recv_sem.at[h, target], (dp, peer))

    def hop_own(h):
        return kv_copy(h, 0, 4, 2, c + 2)

    def pair_own(h):
        return kv_copy(h, 1, 4, 3, c + 1)

    def hop_relay(h):
        return kv_copy(h, 2, 2, 0, c + 2)

    def pair_near_up(h):
        return kv_copy(h, 3, 2, 1, c + 1)

    def pair_near_down(h):
        return kv_copy(h, 3, 2, 3, c - 1)

    def pair_far_down(h):
        return kv_copy(h, 4, 0, 1, c - 1)

    def back_own(h):
        return push(kv_buf.at[h, own], back_buf.at[h], send_sem.at[h, 5], back_recv.at[h],
                    (dp, ahead(c, 6, 8)))

    def back_relay(h):
        return push(back_buf.at[h], kv_buf.at[h, 0], send_sem.at[h, 6], recv_sem.at[h, 0],
                    (dp, ahead(c, 6, 8)))

    def is_back(h):
        return h % 2 == 1

    outer = jnp.logical_or(y == 0, y == 3)

    def send_own(h, carry):
        kv_load(h, 0).wait()
        kv_load(h, 1).wait()

        @pl.when(y < 3)
        def _():
            hop_own(h).start()

        @pl.when(core == 0)
        def _():
            pair_own(h).start()

        @pl.when(jnp.logical_and(is_back(h), y < 2))
        def _():
            back_own(h).start()
        return carry

    send_own(0, 0)
    for j in range(1, BLOCKS):
        @pl.when(c + j < 8)
        def _():
            doc_copy(j).start()
    lax.fori_loop(1, KV, send_own, 0)

    rank_rows = pl.ds(pl.multiple_of(core * HALF_ROWS, HALF_ROWS), HALF_ROWS)
    block_cols = pl.ds(pl.multiple_of(x * XCOLS, HEAD), XCOLS)
    small[1].wait()
    a_roll[:, 512:WIN] = jnp.zeros((RANK, WIN - 512), F32)
    a_roll[:, 0:SHARD] = a_ref[...]
    offsets = (0, 96, 64, 32)
    for quarter in range(1, 4):
        @pl.when(z % 4 == quarter)
        def _():
            a_roll[...] = pltpu.roll(a_roll[...], offsets[quarter], axis=1)
    z_in[z] = a_roll[rank_rows, :].astype(BF16)

    def fz_copy(d):
        return push(z_in.at[z], z_in.at[z], fz_send.at[d - 1], fz_recv.at[d - 1],
                    at(x, ahead(z, d, NZ), y, core))

    def fz_wait(d):
        src = ahead(z, NZ - d, NZ)
        push(z_in.at[src], z_in.at[src], fz_send.at[d - 1], fz_recv.at[d - 1],
             at(x, ahead(z, d, NZ), y, core)).wait_recv()

    for d in range(1, NZ):
        fz_copy(d).start()

    def fx_copy(d):
        return push(f_ref.at[rank_rows, block_cols], f_ref.at[rank_rows, block_cols],
                    fx_send.at[d - 1], fx_recv.at[d - 1], at(ahead(x, d, NX), z, y, core))

    def section(xx):
        return pl.ds(pl.multiple_of(xx * XCOLS, HEAD), XCOLS)

    def fx_wait(d):
        src = ahead(x, NX - d, NX)
        push(f_ref.at[rank_rows, section(src)], f_ref.at[rank_rows, section(src)],
             fx_send.at[d - 1], fx_recv.at[d - 1], at(ahead(x, d, NX), z, y, core)).wait_recv()

    other_rows = pl.ds(pl.multiple_of((1 - core) * HALF_ROWS, HALF_ROWS), HALF_ROWS)

    def fc_copy(d):
        src = ahead(x, NX - d, NX)
        return push(f_ref.at[rank_rows, section(src)], f_ref.at[rank_rows, section(src)],
                    fc_send.at[d], fc_recv.at[d], at(x, z, y, 1 - core))

    def fc_wait(d):
        src = ahead(x, NX - d, NX)
        push(f_ref.at[other_rows, section(src)], f_ref.at[other_rows, section(src)],
             fc_send.at[d], fc_recv.at[d], at(x, z, y, 1 - core)).wait_recv()

    def gather_block():
        for d in range(1, NZ):
            fz_wait(d)
        for quad in range(2):
            w = [z_in[quad * 4 + i] for i in range(4)]
            pieces = [
                w[0][:, 0:512], w[0][:, 512:640] + w[1][:, 0:128],
                w[1][:, 128:640], w[1][:, 640:768] + w[2][:, 0:128],
                w[2][:, 128:640], w[2][:, 640:768] + w[3][:, 0:128],
                w[3][:, 128:640],
            ]
            where = pl.ds(pl.multiple_of(x * XCOLS + quad * HALF, HEAD), HALF)
            f_ref[rank_rows, where] = jnp.concatenate(pieces, axis=1)
        for d in range(1, NX):
            fx_copy(d).start()
        fc_copy(0).start()

    def relay_near(h):
        @pl.when(y >= 1)
        def _():
            hop_own(h).wait_recv()

            @pl.when(jnp.logical_and(jnp.logical_not(is_back(h)), y < 3))
            def _():
                hop_relay(h).start()

            @pl.when(core == 0)
            def _():
                pair_near_up(h).start()

            @pl.when(core == 1)
            def _():
                pair_near_down(h).start()

        @pl.when(jnp.logical_and(is_back(h), outer))
        def _():
            back_own(h).wait_recv()
            back_relay(h).start()

    def relay_far(h):
        @pl.when(y >= 2)
        def _():
            hop_relay(h).wait_recv()

            @pl.when(core == 1)
            def _():
                pair_far_down(h).start()

    def arrive(h):
        @pl.when(jnp.logical_or(core == 1, y >= 1))
        def _():
            pair_own(h).wait_recv()

        @pl.when(jnp.logical_or(y >= 2, jnp.logical_and(core == 1, y >= 1)))
        def _():
            pair_far_down(h).wait_recv()

    relay_near(0)
    relay_near(1)
    small[2].wait()
    lw_t[...] = jnp.broadcast_to(lw_ref[...].astype(F32), (ROWS, ROWS)).T
    for slot in range(own):
        @pl.when(c + slot >= own)
        def _():
            doc_copy(own - slot).wait_recv()
    doc_col = jnp.broadcast_to(doc_buf[own][0:1, :], (ROWS, ROWS)).T
    row_pos = lax.broadcasted_iota(jnp.int32, (ROWS, ROWS), 0)
    key_pos = lax.broadcasted_iota(jnp.int32, (ROWS, ROWS), 1)
    for slot in range(BLOCKS):
        allowed = jnp.broadcast_to(doc_buf[slot][0:1, :], (ROWS, ROWS)) == doc_col
        if slot == own:
            allowed = jnp.logical_and(allowed, key_pos <= row_pos)
        bias[:, slot * ROWS:(slot + 1) * ROWS] = jnp.where(allowed, 0.0, NEG)
    small[3].wait()
    relay_far(0)

    scale = 1.0 / HEAD ** 0.5
    fold = scale * float(np.log2(np.e))
    part_heads = 4

    def one_group(h, carry):
        @pl.when(h + 2 < KV)
        def _():
            relay_near(h + 2)

        @pl.when(h + 1 < KV)
        def _():
            relay_far(h + 1)

        @pl.when(h == 2)
        def _():
            gather_block()

        q_load(h).wait()
        g_load(h).wait()
        arrive(h)
        keys = kv_buf[h, :, 0].reshape(WINDOW, HEAD)
        vals = kv_buf[h, :, 1].reshape(WINDOW, HEAD)

        def head_cols(i):
            return pl.ds(pl.multiple_of(h * GROUP * HEAD + i * HEAD, HEAD), HEAD)

        def front(part):
            heads = range(part * part_heads, (part + 1) * part_heads)
            queries = jnp.concatenate([q_ref[:, head_cols(i)] for i in heads], axis=0)
            weighted = jnp.concatenate(
                [(g_ref[:, head_cols(i)].astype(F32) * lw_t[...]).astype(BF16) for i in heads],
                axis=0)
            w_buf[part] = weighted
            return dot(queries, keys, NT), dot(weighted, vals, NT)

        parts = GROUP // part_heads
        ready = front(0)
        dv = None
        for part in range(parts):
            scores, dprobs = ready
            if part + 1 < parts:
                ready = front(part + 1)
            probs_b, dscores = [], []
            for t in range(part_heads):
                rows = slice(t * ROWS, (t + 1) * ROWS)
                masked = scores[rows] + bias[...]
                top = jnp.max(masked, axis=1, keepdims=True)
                expo = jnp.exp2((masked - top) * fold)
                probs = expo * (1.0 / jnp.sum(expo, axis=1, keepdims=True))
                dp_rows = dprobs[rows]
                delta = jnp.sum(probs * dp_rows, axis=1, keepdims=True)
                probs_b.append(probs.astype(BF16))
                dscores.append((probs * (dp_rows - delta)).astype(BF16))
            dq = dot(jnp.concatenate(dscores, axis=0), keys, NN) * scale
            for t in range(part_heads):
                rot = dq[t * ROWS:(t + 1) * ROWS].astype(BF16).astype(F32)
                dq_ref[:, head_cols(part * part_heads + t)] = (
                    rot * table[0] + pltpu.roll(rot, HEAD // 2, axis=1) * table[1]).astype(BF16)
            more = dot(turn(w_buf[part]), jnp.concatenate(probs_b, axis=0), NN)
            dv = more if dv is None else dv + more
        dv_ref[cols_of(h, HEAD), :] = dv.astype(BF16)
        return carry

    lax.fori_loop(0, KV, one_group, 0)

    for d in range(1, NX):
        fx_wait(d)
        fc_copy(d).start()
    small[4].wait()
    for d in range(NX):
        fc_wait(d)

    def low_copy(j):
        return push(low_buf.at[own], low_buf.at[own - j], low_send.at[j - 1],
                    low_recv.at[own - j], (dp, c + j))

    def mid_copy(j):
        return push(mid_part.at[own - j], mid_buf.at[j - 1], mid_send.at[j - 1],
                    mid_recv.at[j - 1], (dp, c - j))

    low_buf[own] = dot(f_ref[:, D:2 * D], x_ref[...], NT).astype(BF16)
    for j in range(1, BLOCKS):
        @pl.when(c + j < 8)
        def _():
            low_copy(j).start()
    piece = dot(f_ref[:, BV:FACT], dv_ref[...], NN)
    for slot in range(BLOCKS):
        mid_part[slot] = piece[:, slot * ROWS:(slot + 1) * ROWS]
    for j in range(1, BLOCKS):
        @pl.when(c >= j)
        def _():
            mid_copy(j).start()

    low_q = dot(f_ref[:, 0:D], x_ref[...], NT).astype(BF16)
    for i in range(KV):
        grad[:, BQ + i * 1024:BQ + (i + 1) * 1024] = dot(
            low_q, dq_ref[:, i * 1024:(i + 1) * 1024], NN)
    for slot in range(own):
        @pl.when(c + slot >= own)
        def _():
            low_copy(own - slot).wait_recv()
    low_window = jnp.concatenate([low_buf[s] for s in range(BLOCKS)], axis=1)
    grad[:, BV:FACT] = dot(low_window, dv_ref[...], NT)

    def core_copy(part_x):
        return push(
            grad.at[:, pl.ds(pl.multiple_of(part_x * XCOLS + (1 - core) * HALF, HEAD), HALF)],
            core_buf.at[part_x], core_send.at[part_x], core_recv.at[part_x],
            at(x, z, y, 1 - core))

    core_copy(3).start()
    mid_q = dot(f_ref[:, BQ:BV], dq_ref[...], NT).astype(BF16)
    for i in range(5):
        cols = slice(i * 1024, (i + 1) * 1024)
        grad[:, cols] = dot(mid_q, x_ref[:, cols], NN)
    core_copy(0).start()
    mid_v = mid_part[own]
    for j in range(1, BLOCKS):
        @pl.when(c + j < 8)
        def _():
            mid_copy(j).wait_recv()
        mid_v = mid_v + mid_buf[j - 1]
    mid_v = mid_v.astype(BF16)
    for i in range(5):
        grad[:, D + i * 1024:D + (i + 1) * 1024] = dot(
            mid_v, x_ref[:, i * 1024:(i + 1) * 1024], NN)
    core_copy(1).start()
    core_copy(2).start()

    def y_rows(yy):
        return pl.ds(pl.multiple_of(yy * 16, 16), 16)

    def y_copy(d, part_x):
        yy = ahead(y, d, NY)
        return push(stage.at[part_x, y_rows(yy), 0:CUT], ry.at[d - 1, part_x],
                    y_send.at[d - 1, part_x], y_recv.at[d - 1, part_x], at(x, z, yy, core))

    def x_copy(d):
        xx = ahead(x, d, NX)
        return push(stage.at[xx, :, CUT:HALF], rx.at[d - 1],
                    x_send.at[d - 1], x_recv.at[d - 1], at(xx, z, y, core))

    for part_x in (3, 0, 1, 2):
        core_copy(part_x).wait_recv()
        mine = grad[:, pl.ds(pl.multiple_of(part_x * XCOLS + core * HALF, HEAD), HALF)]
        stage[part_x] = (mine + core_buf[part_x]).astype(BF16)
        for d in range(1, NY):
            y_copy(d, part_x).start()
        for d in range(1, NX):
            @pl.when(ahead(x, d, NX) == part_x)
            def _():
                x_copy(d).start()

    def x2_copy(d):
        return push(s2a.at[d - 1], rx2.at[d - 1], x2_send.at[d - 1], x2_recv.at[d - 1],
                    at(ahead(x, d, NX), z, y, core))

    def y2_copy(d):
        return push(s2b.at[d - 1], ry2.at[d - 1], y2_send.at[d - 1], y2_recv.at[d - 1],
                    at(x, z, ahead(y, d, NY), core))

    for part_x in (3, 0, 1, 2):
        for d in range(1, NY):
            y_copy(d, part_x).wait_recv()
    for d in (1, 2, 3, 0):
        xx = ahead(x, d, NX)
        value = stage[xx, y_rows(y), 0:CUT].astype(F32)
        for e in range(NY - 1):
            value = value + ry[e, xx].astype(F32)
        if d:
            s2a[d - 1] = value.astype(BF16)
            x2_copy(d).start()
        else:
            total[:, 0:CUT] = value
    for d in range(1, NX):
        x_copy(d).wait_recv()
    for d in (1, 2, 3, 0):
        yy = ahead(y, d, NY)
        value = stage[x, y_rows(yy), CUT:HALF].astype(F32)
        for e in range(NX - 1):
            value = value + rx[e, y_rows(yy), :].astype(F32)
        if d:
            s2b[d - 1] = value.astype(BF16)
            y2_copy(d).start()
        else:
            total[:, CUT:HALF] = value
    for d in range(1, NX):
        x2_copy(d).wait_recv()
    value = total[:, 0:CUT]
    for e in range(NX - 1):
        value = value + rx2[e].astype(F32)
    total[:, 0:CUT] = value
    for d in range(1, NY):
        y2_copy(d).wait_recv()
    value = total[:, CUT:HALF]
    for e in range(NY - 1):
        value = value + ry2[e].astype(F32)
    total[:, CUT:HALF] = value
    z_out[...] = total[...].astype(BF16)

    starts = (0, 512, 1152, 1664)

    def z_copy(quarter, slot):
        return push(z_out.at[:, starts[quarter]:starts[quarter] + WIN], rz.at[slot],
                    z_send.at[quarter], z_recv.at[slot], at(x, core * 4 + quarter, y, core))

    for quarter in range(4):
        @pl.when(core * 4 + quarter != z)
        def _():
            z_copy(quarter, z).start()

    def full_copy(j):
        return push(full.at[y_rows(y)], full.at[y_rows(y)], f_send.at[j - 1],
                    f_recv.at[y], (dp, ahead(c, j, 8)))

    holder = z // 4

    @pl.when(core == holder)
    def _():
        for quarter in range(4):
            @pl.when(z % 4 == quarter)
            def _():
                z_sum[...] = total[:, starts[quarter]:starts[quarter] + WIN]
        value = z_sum[...]
        for s in range(1, NZ):
            slot = ahead(z, s, NZ)
            z_copy(0, slot).wait_recv()
            value = value + rz[slot].astype(F32)
        for quarter in range(4):
            @pl.when(z % 4 == quarter)
            def _():
                shift = quarter * SHARD - starts[quarter]
                moved = pltpu.roll(value, WIN - shift, axis=1) if shift else value
                full[y_rows(y), :] = moved[:, 0:640]
        for j in range(1, 8):
            full_copy(j).start()

    def row_wait(yy):
        pltpu.make_async_remote_copy(
            src_ref=full.at[y_rows(yy)], dst_ref=full.at[y_rows(yy)], send_sem=f_send.at[0],
            recv_sem=f_recv.at[yy], device_id=(dp, ahead(c, 1, 8)),
            device_id_type=MESH).wait_recv()

    for d in range(1, NY):
        row_wait(ahead(y, d, NY))

    @pl.when(core != holder)
    def _():
        row_wait(y)

    out_ref[...] = full[...] * (ADAPTER_SCALE / (NX * NZ))

    for j in range(1, BLOCKS):
        @pl.when(c + j < 8)
        def _():
            doc_copy(j).wait_send()
            low_copy(j).wait_send()

        @pl.when(c >= j)
        def _():
            mid_copy(j).wait_send()

    def drain(h, carry):
        @pl.when(y < 3)
        def _():
            hop_own(h).wait_send()

        @pl.when(core == 0)
        def _():
            pair_own(h).wait_send()

        @pl.when(jnp.logical_and(is_back(h), y < 2))
        def _():
            back_own(h).wait_send()

        @pl.when(jnp.logical_and(is_back(h), outer))
        def _():
            back_relay(h).wait_send()

        @pl.when(y >= 1)
        def _():
            pair_near_up(h).wait_send()

        @pl.when(jnp.logical_and(jnp.logical_not(is_back(h)), jnp.logical_and(y >= 1, y < 3)))
        def _():
            hop_relay(h).wait_send()

        @pl.when(jnp.logical_and(y >= 2, core == 1))
        def _():
            pair_far_down(h).wait_send()
        return carry

    lax.fori_loop(0, KV, drain, 0)
    for d in range(1, NZ):
        fz_copy(d).wait_send()
    for d in range(1, NX):
        fx_copy(d).wait_send()
    for d in range(NX):
        fc_copy(d).wait_send()
    for part_x in range(NX):
        core_copy(part_x).wait_send()
        for d in range(1, NY):
            y_copy(d, part_x).wait_send()
    for d in range(1, NX):
        x_copy(d).wait_send()
        x2_copy(d).wait_send()
        y2_copy(d).wait_send()
    for quarter in range(4):
        @pl.when(core * 4 + quarter != z)
        def _():
            z_copy(quarter, z).wait_send()

    @pl.when(core == holder)
    def _():
        for j in range(1, 8):
            full_copy(j).wait_send()


def reduced_gradient(q, g, lw, docs, k, v, x, adapter):
    hbm = pl.BlockSpec(memory_space=pltpu.HBM)
    dma = pltpu.SemaphoreType.DMA
    mem = pltpu.VMEM
    return pl.pallas_call(
        kernel,
        out_shape=jax.ShapeDtypeStruct((RANK, 640), F32),
        in_specs=[hbm] * 9,
        out_specs=pl.BlockSpec(memory_space=pltpu.VMEM),
        scratch_shapes=[
            mem((ROWS, QW), BF16), mem((ROWS, QW), BF16),
            mem((1, ROWS), jnp.int32), mem((1, ROWS), jnp.int32),
            mem((ROWS, D), BF16), mem((RANK, SHARD), F32), mem((2, ROWS, HEAD), F32),
            mem((KV, BLOCKS, 2, ROWS, HEAD), BF16), mem((KV, 2, ROWS, HEAD), BF16),
            mem((BLOCKS, 8, ROWS), F32), mem((ROWS, WINDOW), F32), mem((ROWS, ROWS), F32),
            mem((2, 4 * ROWS, HEAD), BF16),
            mem((ROWS, QW), BF16), mem((KV * HEAD, WINDOW), BF16),
            mem((RANK, WIN), F32), mem((NZ, HALF_ROWS, WIN), BF16), mem((RANK, FACT), BF16),
            mem((RANK, FACT), F32), mem((BLOCKS, RANK, ROWS), BF16),
            mem((BLOCKS, RANK, ROWS), F32), mem((BLOCKS - 1, RANK, ROWS), F32),
            mem((NX, RANK, HALF), F32), mem((NX, RANK, HALF), BF16),
            mem((NY - 1, NX, 16, CUT), BF16), mem((NX - 1, RANK, REST), BF16),
            mem((NX - 1, 16, CUT), BF16), mem((NY - 1, 16, REST), BF16),
            mem((NY - 1, 16, REST), BF16), mem((NX - 1, 16, CUT), BF16),
            mem((16, HALF), F32), mem((16, HALF), BF16), mem((NZ, 16, WIN), BF16),
            mem((16, WIN), F32), mem((RANK, 640), F32),
            dma((5,)), dma((KV,)), dma((KV,)), dma((KV, 2)), dma((4,)), dma((4,)),
            dma((KV, 7)), dma((KV, 4)), dma((KV,)),
            dma((7,)), dma((7,)), dma((3,)), dma((3,)), dma((4,)), dma((4,)),
            dma((4,)), dma((4,)), dma((4,)), dma((4,)), dma((4,)), dma((4,)),
            dma((3, 4)), dma((3, 4)), dma((3,)), dma((3,)),
            dma((3,)), dma((3,)), dma((3,)), dma((3,)),
            dma((4,)), dma((8,)), dma((7,)), dma((4,)),
        ],
        compiler_params=pltpu.CompilerParams(
            collective_id=0, has_side_effects=True, vmem_limit_bytes=60 * 1024 * 1024),
        cost_estimate=pl.CostEstimate(
            flops=8 * 64 * WINDOW * ROWS * HEAD + 4 * FACT * RANK * ROWS,
            bytes_accessed=10_000_000, transcendentals=64 * WINDOW * ROWS),
        name="layer_back",
    )(q, g, lw, docs, k, v, x, adapter, jnp.asarray(rope_tables()))


def per_device(
    normed_input, queries, keys, values, out_grad, loss_weight, doc_ids, adapter, moment1, moment2
):
    gradient = reduced_gradient(
        queries[0], out_grad[0], loss_weight, doc_ids, keys[0], values[0], normed_input[0],
        adapter)[:, 0:SHARD]
    new_m = BETA_ONE * moment1 + (1.0 - BETA_ONE) * gradient
    new_v = BETA_TWO * moment2 + (1.0 - BETA_TWO) * gradient * gradient
    corr_one = 1.0 - BETA_ONE ** STEP_COUNT
    corr_two = 1.0 - BETA_TWO ** STEP_COUNT
    return (new_m, new_v, new_m / corr_one / (jnp.sqrt(new_v / corr_two) + ADAM_EPS))


def solution(mesh):
    in_specs = (
        P("dp", "ctx", None),
        P("dp", "ctx", None),
        P("dp", "ctx", None),
        P("dp", "ctx", None),
        P("dp", "ctx", None),
        P("dp", "ctx"),
        P("dp", "ctx"),
        P(None, "dp"),
        P(None, "dp"),
        P(None, "dp"),
    )
    out_specs = (P(None, "dp"), P(None, "dp"), P(None, "dp"))
    return jax.shard_map(
        per_device, mesh=mesh, in_specs=in_specs, out_specs=out_specs, check_vma=False
    )
```

```python
import functools

import jax
import jax.numpy as jnp
import numpy as np
from jax import lax
from jax.experimental import pallas as pl
from jax.experimental.pallas import tpu as pltpu
from jax.sharding import PartitionSpec as P

HEAD = 128
GROUP = 8
KV = 8
D = 5120
RANK = 64
ROWS = 128
BLOCKS = 5
WINDOW = BLOCKS * ROWS
QW = KV * GROUP * HEAD
FACT = 2 * D + QW + KV * HEAD
BQ = 2 * D
BV = BQ + QW
NX, NZ, NY, NC = 4, 8, 4, 2
SHARD = FACT // (NX * NZ)
XCOLS = FACT // NX
HALF = XCOLS // 2
HALF_ROWS = RANK // 2
CUT = 1152
REST = HALF - CUT
WIN = 768

THETA = 1000000.0
ADAPTER_SCALE = 2.0
BETA_ONE = 0.9
BETA_TWO = 0.95
ADAM_EPS = 1e-08
STEP_COUNT = 10
NEG = -1e30
MESH = pl.DeviceIdType.MESH
NT = (((1,), (1,)), ((), ()))
NN = (((1,), (0,)), ((), ()))
F32 = jnp.float32
BF16 = jnp.bfloat16


def rope_tables():
    freq = THETA ** (-(np.arange(HEAD // 2, dtype=np.float64) * 2.0 / HEAD))
    angle = np.arange(NY * NC * ROWS, dtype=np.float64)[:, None] * freq[None, :]
    cosine, sine = np.cos(angle), np.sin(angle)
    both = np.stack(
        [np.concatenate([cosine, cosine], axis=1), np.concatenate([sine, -sine], axis=1)])
    return both.reshape(2, NY * NC, ROWS, HEAD).transpose(1, 0, 2, 3).astype(np.float32)


def dot(a, b, dims):
    return lax.dot_general(a, b, dims, preferred_element_type=F32)


def turn(a):
    return a.astype(F32).T.astype(BF16)


def kernel(
    q_hbm, g_hbm, lw_hbm, docs_hbm, k_hbm, v_hbm, x_hbm, a_hbm, table_hbm,
    out_ref,
    q_ref, g_ref, lw_ref, docs_ref, x_ref, a_ref, table,
    kv_buf, back_buf, doc_buf, bias, lw_t, w_buf, wt_buf, dq_ref, dv_ref,
    a_roll, z_in, f_ref,
    grad, low_buf, low_q_ref, mid_part, mid_buf, core_out, core_buf, stage, ry, rx, s2a, s2b, ry2, rx2,
    total, z_out, rz, z_sum, full,
    in_sem, q_sem, g_sem, kv_sem, doc_send, doc_recv, send_sem, recv_sem, back_recv,
    fz_send, fz_recv, fx_send, fx_recv, fc_send, fc_recv,
    low_send, low_recv, mid_send, mid_recv, core_send, core_recv,
    y_send, y_recv, x_send, x_recv, x2_send, x2_recv, y2_send, y2_recv,
    z_send, z_recv, f_send, f_recv,
):
    dp = lax.axis_index("dp")
    c = lax.axis_index("ctx")
    x, z = dp // NZ, dp % NZ
    y, core = c // 2, c % 2
    own = BLOCKS - 1

    def at(xx, zz, yy, cc):
        return (xx * NZ + zz, yy * 2 + cc)

    def ahead(value, step, size):
        return (value + step) % size

    def push(src, dst, send, recv, peer):
        return pltpu.make_async_remote_copy(
            src_ref=src, dst_ref=dst, send_sem=send, recv_sem=recv,
            device_id=peer, device_id_type=MESH)

    def cols_of(h, width):
        return pl.ds(pl.multiple_of(h * width, width), width)

    def kv_load(h, which):
        source = k_hbm if which == 0 else v_hbm
        return pltpu.make_async_copy(
            source.at[:, cols_of(h, HEAD)], kv_buf.at[h, own, which], kv_sem.at[h, which])

    def q_load(h):
        return pltpu.make_async_copy(
            q_hbm.at[:, cols_of(h, 1024)], q_ref.at[:, cols_of(h, 1024)], q_sem.at[h])

    def g_load(h):
        return pltpu.make_async_copy(
            g_hbm.at[:, cols_of(h, 1024)], g_ref.at[:, cols_of(h, 1024)], g_sem.at[h])

    small = [
        pltpu.make_async_copy(docs_hbm, docs_ref, in_sem.at[0]),
        pltpu.make_async_copy(a_hbm, a_ref, in_sem.at[1]),
        pltpu.make_async_copy(lw_hbm, lw_ref, in_sem.at[2]),
        pltpu.make_async_copy(table_hbm.at[c], table, in_sem.at[3]),
        pltpu.make_async_copy(x_hbm, x_ref, in_sem.at[4]),
    ]
    barrier = pltpu.get_barrier_semaphore()
    peers = [(dp, ahead(c, j, 8)) for j in range(1, 8)]
    peers += [at(ahead(x, d, NX), z, y, core) for d in range(1, NX)]
    peers += [at(x, ahead(z, d, NZ), y, core) for d in range(1, NZ)]
    for peer in peers:
        pl.semaphore_signal(barrier, inc=1, device_id=peer, device_id_type=MESH)
    small[0].start()
    small[1].start()

    def load_kv(h, carry):
        kv_load(h, 0).start()
        kv_load(h, 1).start()
        return carry

    lax.fori_loop(0, KV, load_kv, 0)
    small[2].start()
    small[3].start()

    def load_qg(h, carry):
        q_load(h).start()
        g_load(h).start()
        return carry

    lax.fori_loop(0, KV, load_qg, 0)
    small[4].start()

    for slot in range(own):
        @pl.when(c + slot < own)
        def _():
            doc_buf[slot] = jnp.full((8, ROWS), -1.0, F32)
            low_buf[slot] = jnp.zeros((RANK, ROWS), BF16)
            for h in range(KV):
                kv_buf[h, slot] = jnp.zeros((2, ROWS, HEAD), BF16)

        @pl.when(c + slot + 1 > 7)
        def _():
            mid_buf[slot] = jnp.zeros((RANK, ROWS), F32)

    small[0].wait()
    doc_buf[own] = jnp.broadcast_to(docs_ref[...].astype(F32), (8, ROWS))
    pl.semaphore_wait(barrier, len(peers))

    def doc_copy(j):
        return push(doc_buf.at[own], doc_buf.at[own - j], doc_send.at[j - 1],
                    doc_recv.at[own - j], (dp, c + j))

    def kv_copy(h, kind, source, target, peer):
        return push(kv_buf.at[h, source], kv_buf.at[h, target], send_sem.at[h, kind],
                    recv_sem.at[h, target], (dp, peer))

    def hop_own(h):
        return kv_copy(h, 0, 4, 2, c + 2)

    def pair_own(h):
        return kv_copy(h, 1, 4, 3, c + 1)

    def hop_relay(h):
        return kv_copy(h, 2, 2, 0, c + 2)

    def pair_near_up(h):
        return kv_copy(h, 3, 2, 1, c + 1)

    def pair_near_down(h):
        return kv_copy(h, 3, 2, 3, c - 1)

    def pair_far_down(h):
        return kv_copy(h, 4, 0, 1, c - 1)

    def back_own(h):
        return push(kv_buf.at[h, own], back_buf.at[h], send_sem.at[h, 5], back_recv.at[h],
                    (dp, ahead(c, 6, 8)))

    def back_relay(h):
        return push(back_buf.at[h], kv_buf.at[h, 0], send_sem.at[h, 6], recv_sem.at[h, 0],
                    (dp, ahead(c, 6, 8)))

    def is_back(h):
        return h % 2 == 1

    outer = jnp.logical_or(y == 0, y == 3)

    def send_own(h, carry):
        kv_load(h, 0).wait()
        kv_load(h, 1).wait()

        @pl.when(y < 3)
        def _():
            hop_own(h).start()

        @pl.when(core == 0)
        def _():
            pair_own(h).start()

        @pl.when(jnp.logical_and(is_back(h), y < 2))
        def _():
            back_own(h).start()
        return carry

    send_own(0, 0)
    for j in range(1, BLOCKS):
        @pl.when(c + j < 8)
        def _():
            doc_copy(j).start()
    send_own(1, 0)

    rank_rows = pl.ds(pl.multiple_of(core * HALF_ROWS, HALF_ROWS), HALF_ROWS)
    small[1].wait()
    a_roll[:, 512:WIN] = jnp.zeros((RANK, WIN - 512), F32)
    a_roll[:, 0:SHARD] = a_ref[...]
    offsets = (0, 96, 64, 32)
    for quarter in range(1, 4):
        @pl.when(z % 4 == quarter)
        def _():
            a_roll[...] = pltpu.roll(a_roll[...], offsets[quarter], axis=1)
    z_in[z] = a_roll[rank_rows, :].astype(BF16)

    span = (slice(0, 16), slice(16, 32))

    def fz_push(src, d, part):
        return push(z_in.at[src, span[part]], z_in.at[src, span[part]],
                    fz_send.at[part, d - 1], fz_recv.at[part, d - 1],
                    at(x, ahead(z, d, NZ), y, core))

    for part in range(2):
        for d in (4, 3, 5, 2, 6, 1, 7):
            fz_push(z, d, part).start()

    def section(xx):
        return pl.ds(pl.multiple_of(xx * XCOLS, HEAD), XCOLS)

    def half_section(xx, part):
        return pl.ds(pl.multiple_of(xx * XCOLS + part * HALF, HEAD), HALF)

    def f_rows(cc, part):
        return pl.ds(pl.multiple_of(cc * HALF_ROWS + part * 16, 16), 16)

    def fx_push(src, d, part):
        where = f_ref.at[f_rows(core, part), section(src)]
        return push(where, where, fx_send.at[part, d - 1], fx_recv.at[part, d - 1],
                    at(ahead(x, d, NX), z, y, core))

    def fc_push(cc, d, part):
        where = f_ref.at[f_rows(cc, part), section(ahead(x, NX - d, NX))]
        return push(where, where, fc_send.at[part, d], fc_recv.at[part, d],
                    at(x, z, y, 1 - core))

    def gather_block(part):
        for d in range(1, NZ):
            fz_push(ahead(z, NZ - d, NZ), d, part).wait_recv()
        for quad in range(2):
            w = [z_in[quad * 4 + i, span[part]] for i in range(4)]
            pieces = [
                w[0][:, 0:512], w[0][:, 512:640] + w[1][:, 0:128],
                w[1][:, 128:640], w[1][:, 640:768] + w[2][:, 0:128],
                w[2][:, 128:640], w[2][:, 640:768] + w[3][:, 0:128],
                w[3][:, 128:640],
            ]
            f_ref[f_rows(core, part), half_section(x, quad)] = jnp.concatenate(pieces, axis=1)
        for d in (2, 1, 3):
            fx_push(x, d, part).start()
        fc_push(core, 0, part).start()

    def gather_pair(part):
        for d in (1, 3, 2):
            fx_push(ahead(x, NX - d, NX), d, part).wait_recv()
            fc_push(core, d, part).start()

    def low_copy(j):
        return push(low_buf.at[own], low_buf.at[own - j], low_send.at[j - 1],
                    low_recv.at[own - j], (dp, c + j))

    def make_low():
        for part in range(2):
            for d in range(NX):
                fc_push(1 - core, d, part).wait_recv()
        small[4].wait()
        both = dot(jnp.concatenate([f_ref[:, D:2 * D], f_ref[:, 0:D]], axis=0), x_ref[...], NT)
        low_buf[own] = both[0:RANK].astype(BF16)
        for j in range(1, BLOCKS):
            @pl.when(c + j < 8)
            def _():
                low_copy(j).start()
        low_q_ref[...] = both[RANK:].astype(BF16)

    def relay_near(h):
        @pl.when(y >= 1)
        def _():
            hop_own(h).wait_recv()

            @pl.when(jnp.logical_and(jnp.logical_not(is_back(h)), y < 3))
            def _():
                hop_relay(h).start()

            @pl.when(core == 0)
            def _():
                pair_near_up(h).start()

            @pl.when(core == 1)
            def _():
                pair_near_down(h).start()

        @pl.when(jnp.logical_and(is_back(h), outer))
        def _():
            back_own(h).wait_recv()
            back_relay(h).start()

    def relay_far(h):
        @pl.when(y >= 2)
        def _():
            hop_relay(h).wait_recv()

            @pl.when(core == 1)
            def _():
                pair_far_down(h).start()

    def arrive(h):
        @pl.when(jnp.logical_or(core == 1, y >= 1))
        def _():
            pair_own(h).wait_recv()

        @pl.when(jnp.logical_or(y >= 2, jnp.logical_and(core == 1, y >= 1)))
        def _():
            pair_far_down(h).wait_recv()

    small[2].wait()
    lw_t[...] = jnp.broadcast_to(lw_ref[...].astype(F32), (ROWS, ROWS)).T

    def weigh(h, carry):
        g_load(h).wait()
        weighted = [
            (g_ref[:, pl.ds(pl.multiple_of(h * 1024 + i * HEAD, HEAD), HEAD)].astype(F32)
             * lw_t[...]).astype(BF16)
            for i in range(GROUP)]
        for i in range(GROUP):
            w_buf[h, i * ROWS:(i + 1) * ROWS] = weighted[i]
            wt_buf[h, :, i * ROWS:(i + 1) * ROWS] = turn(weighted[i])
        return carry

    lax.fori_loop(0, 3, weigh, 0)
    relay_near(0)
    send_own(2, 0)
    relay_near(1)
    send_own(3, 0)
    lax.fori_loop(3, KV, weigh, 0)
    for slot in range(own):
        @pl.when(c + slot >= own)
        def _():
            doc_copy(own - slot).wait_recv()
    doc_col = jnp.broadcast_to(doc_buf[own][0:1, :], (ROWS, ROWS)).T
    row_pos = lax.broadcasted_iota(jnp.int32, (ROWS, ROWS), 0)
    key_pos = lax.broadcasted_iota(jnp.int32, (ROWS, ROWS), 1)
    for slot in range(BLOCKS):
        allowed = jnp.broadcast_to(doc_buf[slot][0:1, :], (ROWS, ROWS)) == doc_col
        block = jnp.where(allowed, 0.0, NEG)
        if slot == 0:
            first_block = block
        elif slot == own:
            bias[:, 0:ROWS] = jnp.where(key_pos <= row_pos, block, first_block)
        else:
            bias[:, slot * ROWS:(slot + 1) * ROWS] = block
    small[3].wait()
    relay_far(0)

    scale = 1.0 / HEAD ** 0.5
    fold = scale * float(np.log2(np.e))
    part_heads = 4

    edge = own * ROWS

    def one_group(h, carry):
        lower = lax.broadcasted_iota(jnp.int32, (ROWS, ROWS), 1) <= lax.broadcasted_iota(
            jnp.int32, (ROWS, ROWS), 0)

        def fold_ends(a):
            return jnp.concatenate(
                [jnp.where(lower, a[:, edge:], a[:, 0:ROWS]), a[:, ROWS:edge]], axis=1)

        def unfold_ends(a):
            ends = a[:, 0:ROWS]
            return jnp.concatenate(
                [jnp.where(lower, 0.0, ends).astype(BF16), a[:, ROWS:].astype(BF16),
                 jnp.where(lower, ends, 0.0).astype(BF16)], axis=1)

        @pl.when(h + 2 < KV)
        def _():
            relay_near(h + 2)

        @pl.when(h + 4 < KV)
        def _():
            send_own(h + 4, 0)

        @pl.when(h + 1 < KV)
        def _():
            relay_far(h + 1)

        @pl.when(h == 1)
        def _():
            gather_block(0)

        @pl.when(h == 2)
        def _():
            gather_block(1)

        @pl.when(h == 5)
        def _():
            gather_pair(0)

        @pl.when(h == 7)
        def _():
            gather_pair(1)

        q_load(h).wait()
        arrive(h)
        keys = kv_buf[h, :, 0].reshape(WINDOW, HEAD)
        vals = kv_buf[h, :, 1].reshape(WINDOW, HEAD)

        def head_cols(i):
            return pl.ds(pl.multiple_of(h * GROUP * HEAD + i * HEAD, HEAD), HEAD)

        def front(part):
            heads = range(part * part_heads, (part + 1) * part_heads)
            queries = jnp.concatenate([q_ref[:, head_cols(i)] for i in heads], axis=0)
            weighted = w_buf[h, part * 512:(part + 1) * 512]
            return dot(queries, keys, NT), dot(weighted, vals, NT)

        parts = GROUP // part_heads
        ready = front(0)
        dv = None
        for part in range(parts):
            scores, dprobs = ready
            if part + 1 < parts:
                ready = front(part + 1)
            probs_b, dscores = [], []
            for t in range(part_heads):
                rows = slice(t * ROWS, (t + 1) * ROWS)
                masked = fold_ends(scores[rows]) + bias[...]
                top = jnp.max(masked, axis=1, keepdims=True)
                expo = jnp.exp2((masked - top) * fold)
                probs = expo * (1.0 / jnp.sum(expo, axis=1, keepdims=True))
                dp_rows = fold_ends(dprobs[rows])
                delta = jnp.sum(probs * dp_rows, axis=1, keepdims=True)
                probs_b.append(unfold_ends(probs))
                dscores.append(unfold_ends(probs * (dp_rows - delta)))
            dq = dot(jnp.concatenate(dscores, axis=0), keys, NN) * scale
            for t in range(part_heads):
                rot = dq[t * ROWS:(t + 1) * ROWS].astype(BF16).astype(F32)
                dq_ref[:, head_cols(part * part_heads + t)] = (
                    rot * table[0] + pltpu.roll(rot, HEAD // 2, axis=1) * table[1]).astype(BF16)
            more = dot(
                wt_buf[h, :, part * 512:(part + 1) * 512], jnp.concatenate(probs_b, axis=0), NN)
            dv = more if dv is None else dv + more
        dv_ref[cols_of(h, HEAD), :] = dv.astype(BF16)
        return carry

    lax.fori_loop(0, KV, one_group, 0)
    make_low()

    def mid_copy(j):
        return push(mid_part.at[own - j], mid_buf.at[j - 1], mid_send.at[j - 1],
                    mid_recv.at[j - 1], (dp, c - j))

    piece = dot(f_ref[:, BV:FACT], dv_ref[...], NN)
    for slot in range(BLOCKS):
        mid_part[slot] = piece[:, slot * ROWS:(slot + 1) * ROWS]
    for j in range(1, BLOCKS):
        @pl.when(c >= j)
        def _():
            mid_copy(j).start()

    def core_copy(part_x):
        return push(core_out.at[part_x], core_buf.at[part_x], core_send.at[part_x],
                    core_recv.at[part_x], at(x, z, y, 1 - core))

    def core_start(part_x):
        theirs = grad[:, pl.ds(
            pl.multiple_of(part_x * XCOLS + (1 - core) * HALF, HEAD), HALF)]
        core_out[part_x] = theirs.astype(BF16)
        core_copy(part_x).start()

    def y_rows(yy):
        return pl.ds(pl.multiple_of(yy * 16, 16), 16)

    def y_copy(d, part_x):
        yy = ahead(y, d, NY)
        return push(stage.at[part_x, y_rows(yy), 0:CUT], ry.at[d - 1, part_x],
                    y_send.at[d - 1, part_x], y_recv.at[d - 1, part_x], at(x, z, yy, core))

    def x_copy(d):
        xx = ahead(x, d, NX)
        return push(stage.at[xx, :, CUT:HALF], rx.at[d - 1],
                    x_send.at[d - 1], x_recv.at[d - 1], at(xx, z, y, core))

    def core_finish(part_x):
        core_copy(part_x).wait_recv()
        mine = grad[:, pl.ds(pl.multiple_of(part_x * XCOLS + core * HALF, HEAD), HALF)]
        stage[part_x] = (mine + core_buf[part_x].astype(F32)).astype(BF16)
        for d in (2, 1, 3):
            y_copy(d, part_x).start()
        for d in range(1, NX):
            @pl.when(ahead(x, d, NX) == part_x)
            def _():
                x_copy(d).start()

    def q_rank_cols(first, last):
        for i in range(first, last, 1024):
            stop = min(i + 1024, last)
            grad[:, BQ + i:BQ + stop] = dot(low_q_ref[...], dq_ref[:, i:stop], NN)

    q_cut = 3 * XCOLS - BQ
    mid_q = dot(f_ref[:, BQ:BV], dq_ref[...], NT).astype(BF16)
    for i in range(5):
        grad[:, i * 1024:(i + 1) * 1024] = dot(mid_q, x_ref[:, i * 1024:(i + 1) * 1024], NN)
    core_start(0)
    q_rank_cols(q_cut, QW)
    for slot in range(own):
        @pl.when(c + slot >= own)
        def _():
            low_copy(own - slot).wait_recv()
    low_window = jnp.concatenate([low_buf[s] for s in range(BLOCKS)], axis=1)
    grad[:, BV:FACT] = dot(low_window, dv_ref[...], NT)
    core_start(3)
    core_finish(0)
    q_rank_cols(0, q_cut)
    mid_v = mid_part[own]
    for j in range(1, BLOCKS):
        @pl.when(c + j < 8)
        def _():
            mid_copy(j).wait_recv()
        mid_v = mid_v + mid_buf[j - 1]
    mid_v = mid_v.astype(BF16)
    for i in (4, 3, 2, 1, 0):
        grad[:, D + i * 1024:D + (i + 1) * 1024] = dot(
            mid_v, x_ref[:, i * 1024:(i + 1) * 1024], NN)
        if i == 4:
            core_start(2)
    core_start(1)
    core_finish(3)
    core_finish(2)
    core_finish(1)

    def x2_copy(d):
        return push(s2a.at[d - 1], rx2.at[d - 1], x2_send.at[d - 1], x2_recv.at[d - 1],
                    at(ahead(x, d, NX), z, y, core))

    def y2_copy(d):
        return push(s2b.at[d - 1], ry2.at[d - 1], y2_send.at[d - 1], y2_recv.at[d - 1],
                    at(x, z, ahead(y, d, NY), core))

    for part_x in (0, 3, 2, 1):
        for d in range(1, NY):
            y_copy(d, part_x).wait_recv()
        value = stage[part_x, y_rows(y), 0:CUT].astype(F32)
        for e in range(NY - 1):
            value = value + ry[e, part_x].astype(F32)

        @pl.when(x == part_x)
        def _():
            total[:, 0:CUT] = value

        for d in range(1, NX):
            @pl.when(ahead(x, d, NX) == part_x)
            def _():
                s2a[d - 1] = value.astype(BF16)
                x2_copy(d).start()

    for d in range(1, NX):
        x_copy(d).wait_recv()
    for d in (1, 2, 3, 0):
        yy = ahead(y, d, NY)
        value = stage[x, y_rows(yy), CUT:HALF].astype(F32)
        for e in range(NX - 1):
            value = value + rx[e, y_rows(yy), :].astype(F32)
        if d:
            s2b[d - 1] = value.astype(BF16)
            y2_copy(d).start()
        else:
            total[:, CUT:HALF] = value
    for d in range(1, NX):
        x2_copy(d).wait_recv()
    value = total[:, 0:CUT]
    for e in range(NX - 1):
        value = value + rx2[e].astype(F32)
    total[:, 0:CUT] = value
    for d in range(1, NY):
        y2_copy(d).wait_recv()
    value = total[:, CUT:HALF]
    for e in range(NY - 1):
        value = value + ry2[e].astype(F32)
    total[:, CUT:HALF] = value
    z_out[...] = total[...].astype(BF16)

    starts = (0, 512, 1152, 1664)

    def z_copy(quarter, slot):
        return push(z_out.at[:, starts[quarter]:starts[quarter] + WIN], rz.at[slot],
                    z_send.at[quarter], z_recv.at[slot], at(x, core * 4 + quarter, y, core))

    for quarter in range(4):
        @pl.when(core * 4 + quarter != z)
        def _():
            z_copy(quarter, z).start()

    def full_copy(j):
        return push(full.at[y_rows(y)], full.at[y_rows(y)], f_send.at[j - 1],
                    f_recv.at[y], (dp, ahead(c, j, 8)))

    holder = z // 4

    @pl.when(core == holder)
    def _():
        for quarter in range(4):
            @pl.when(z % 4 == quarter)
            def _():
                z_sum[...] = total[:, starts[quarter]:starts[quarter] + WIN]
        value = z_sum[...]
        for s in range(1, NZ):
            slot = ahead(z, s, NZ)
            z_copy(0, slot).wait_recv()
            value = value + rz[slot].astype(F32)
        for quarter in range(4):
            @pl.when(z % 4 == quarter)
            def _():
                shift = quarter * SHARD - starts[quarter]
                moved = pltpu.roll(value, WIN - shift, axis=1) if shift else value
                full[y_rows(y), :] = moved[:, 0:640]
        for j in range(1, 8):
            full_copy(j).start()

    def row_wait(yy):
        pltpu.make_async_remote_copy(
            src_ref=full.at[y_rows(yy)], dst_ref=full.at[y_rows(yy)], send_sem=f_send.at[0],
            recv_sem=f_recv.at[yy], device_id=(dp, ahead(c, 1, 8)),
            device_id_type=MESH).wait_recv()

    for d in range(1, NY):
        row_wait(ahead(y, d, NY))

    @pl.when(core != holder)
    def _():
        row_wait(y)

    out_ref[...] = full[...] * (ADAPTER_SCALE / (NX * NZ))

    for j in range(1, BLOCKS):
        @pl.when(c + j < 8)
        def _():
            doc_copy(j).wait_send()
            low_copy(j).wait_send()

        @pl.when(c >= j)
        def _():
            mid_copy(j).wait_send()

    def drain(h, carry):
        @pl.when(y < 3)
        def _():
            hop_own(h).wait_send()

        @pl.when(core == 0)
        def _():
            pair_own(h).wait_send()

        @pl.when(jnp.logical_and(is_back(h), y < 2))
        def _():
            back_own(h).wait_send()

        @pl.when(jnp.logical_and(is_back(h), outer))
        def _():
            back_relay(h).wait_send()

        @pl.when(y >= 1)
        def _():
            pair_near_up(h).wait_send()

        @pl.when(jnp.logical_and(jnp.logical_not(is_back(h)), jnp.logical_and(y >= 1, y < 3)))
        def _():
            hop_relay(h).wait_send()

        @pl.when(jnp.logical_and(y >= 2, core == 1))
        def _():
            pair_far_down(h).wait_send()
        return carry

    lax.fori_loop(0, KV, drain, 0)
    for part in range(2):
        for d in range(1, NZ):
            fz_push(z, d, part).wait_send()
        for d in range(1, NX):
            fx_push(x, d, part).wait_send()
        for d in range(NX):
            fc_push(core, d, part).wait_send()
    for part_x in range(NX):
        core_copy(part_x).wait_send()
        for d in range(1, NY):
            y_copy(d, part_x).wait_send()
    for d in range(1, NX):
        x_copy(d).wait_send()
        x2_copy(d).wait_send()
        y2_copy(d).wait_send()
    for quarter in range(4):
        @pl.when(core * 4 + quarter != z)
        def _():
            z_copy(quarter, z).wait_send()

    @pl.when(core == holder)
    def _():
        for j in range(1, 8):
            full_copy(j).wait_send()


def reduced_gradient(q, g, lw, docs, k, v, x, adapter):
    hbm = pl.BlockSpec(memory_space=pltpu.HBM)
    dma = pltpu.SemaphoreType.DMA
    mem = pltpu.VMEM
    return pl.pallas_call(
        kernel,
        out_shape=jax.ShapeDtypeStruct((RANK, 640), F32),
        in_specs=[hbm] * 9,
        out_specs=pl.BlockSpec(memory_space=pltpu.VMEM),
        scratch_shapes=[
            mem((ROWS, QW), BF16), mem((ROWS, QW), BF16),
            mem((1, ROWS), jnp.int32), mem((1, ROWS), jnp.int32),
            mem((ROWS, D), BF16), mem((RANK, SHARD), F32), mem((2, ROWS, HEAD), F32),
            mem((KV, BLOCKS, 2, ROWS, HEAD), BF16), mem((KV, 2, ROWS, HEAD), BF16),
            mem((BLOCKS, 8, ROWS), F32), mem((ROWS, WINDOW - ROWS), F32), mem((ROWS, ROWS), F32),
            mem((KV, GROUP * ROWS, HEAD), BF16), mem((KV, HEAD, GROUP * ROWS), BF16),
            mem((ROWS, QW), BF16), mem((KV * HEAD, WINDOW), BF16),
            mem((RANK, WIN), F32), mem((NZ, HALF_ROWS, WIN), BF16), mem((RANK, FACT), BF16),
            mem((RANK, FACT), F32), mem((BLOCKS, RANK, ROWS), BF16), mem((RANK, ROWS), BF16),
            mem((BLOCKS, RANK, ROWS), F32), mem((BLOCKS - 1, RANK, ROWS), F32),
            mem((NX, RANK, HALF), BF16), mem((NX, RANK, HALF), BF16), mem((NX, RANK, HALF), BF16),
            mem((NY - 1, NX, 16, CUT), BF16), mem((NX - 1, RANK, REST), BF16),
            mem((NX - 1, 16, CUT), BF16), mem((NY - 1, 16, REST), BF16),
            mem((NY - 1, 16, REST), BF16), mem((NX - 1, 16, CUT), BF16),
            mem((16, HALF), F32), mem((16, HALF), BF16), mem((NZ, 16, WIN), BF16),
            mem((16, WIN), F32), mem((RANK, 640), F32),
            dma((5,)), dma((KV,)), dma((KV,)), dma((KV, 2)), dma((4,)), dma((4,)),
            dma((KV, 7)), dma((KV, 4)), dma((KV,)),
            dma((2, 7)), dma((2, 7)), dma((2, 3)), dma((2, 3)), dma((2, 4)), dma((2, 4)),
            dma((4,)), dma((4,)), dma((4,)), dma((4,)), dma((4,)), dma((4,)),
            dma((3, 4)), dma((3, 4)), dma((3,)), dma((3,)),
            dma((3,)), dma((3,)), dma((3,)), dma((3,)),
            dma((4,)), dma((8,)), dma((7,)), dma((4,)),
        ],
        compiler_params=pltpu.CompilerParams(
            collective_id=0, has_side_effects=True, vmem_limit_bytes=60 * 1024 * 1024),
        cost_estimate=pl.CostEstimate(
            flops=8 * 64 * WINDOW * ROWS * HEAD + 4 * FACT * RANK * ROWS,
            bytes_accessed=10_000_000, transcendentals=64 * WINDOW * ROWS),
        name="layer_back",
    )(q, g, lw, docs, k, v, x, adapter, jnp.asarray(rope_tables()))


def per_device(
    normed_input, queries, keys, values, out_grad, loss_weight, doc_ids, adapter, moment1, moment2
):
    gradient = reduced_gradient(
        queries[0], out_grad[0], loss_weight, doc_ids, keys[0], values[0], normed_input[0],
        adapter)[:, 0:SHARD]
    new_m = BETA_ONE * moment1 + (1.0 - BETA_ONE) * gradient
    new_v = BETA_TWO * moment2 + (1.0 - BETA_TWO) * gradient * gradient
    corr_one = 1.0 - BETA_ONE ** STEP_COUNT
    corr_two = 1.0 - BETA_TWO ** STEP_COUNT
    return (new_m, new_v, new_m / corr_one / (jnp.sqrt(new_v / corr_two) + ADAM_EPS))


def solution(mesh):
    in_specs = (
        P("dp", "ctx", None),
        P("dp", "ctx", None),
        P("dp", "ctx", None),
        P("dp", "ctx", None),
        P("dp", "ctx", None),
        P("dp", "ctx"),
        P("dp", "ctx"),
        P(None, "dp"),
        P(None, "dp"),
        P(None, "dp"),
    )
    out_specs = (P(None, "dp"), P(None, "dp"), P(None, "dp"))
    return jax.shard_map(
        per_device, mesh=mesh, in_specs=in_specs, out_specs=out_specs, check_vma=False
    )
```

```python
import functools

import jax
import jax.numpy as jnp
import numpy as np
from jax import lax
from jax.experimental import pallas as pl
from jax.experimental.pallas import tpu as pltpu
from jax.sharding import PartitionSpec as P

HEAD = 128
GROUP = 8
KV = 8
D = 5120
RANK = 64
ROWS = 128
BLOCKS = 5
WINDOW = BLOCKS * ROWS
QW = KV * GROUP * HEAD
FACT = 2 * D + QW + KV * HEAD
BQ = 2 * D
BV = BQ + QW
NX, NZ, NY, NC = 4, 8, 4, 2
SHARD = FACT // (NX * NZ)
XCOLS = FACT // NX
HALF = XCOLS // 2
HALF_ROWS = RANK // 2
CUT = 1408
REST = HALF - CUT
WIN = 768

THETA = 1000000.0
ADAPTER_SCALE = 2.0
BETA_ONE = 0.9
BETA_TWO = 0.95
ADAM_EPS = 1e-08
STEP_COUNT = 10
NEG = -1e30
MESH = pl.DeviceIdType.MESH
NT = (((1,), (1,)), ((), ()))
NN = (((1,), (0,)), ((), ()))
F32 = jnp.float32
BF16 = jnp.bfloat16


def rope_tables():
    freq = THETA ** (-(np.arange(HEAD // 2, dtype=np.float64) * 2.0 / HEAD))
    angle = np.arange(NY * NC * ROWS, dtype=np.float64)[:, None] * freq[None, :]
    cosine, sine = np.cos(angle), np.sin(angle)
    both = np.stack(
        [np.concatenate([cosine, cosine], axis=1), np.concatenate([sine, -sine], axis=1)])
    return both.reshape(2, NY * NC, ROWS, HEAD).transpose(1, 0, 2, 3).astype(np.float32)


def dot(a, b, dims):
    return lax.dot_general(a, b, dims, preferred_element_type=F32)


def turn(a):
    return a.astype(F32).T.astype(BF16)


def kernel(
    q_hbm, g_hbm, lw_hbm, docs_hbm, k_hbm, v_hbm, x_hbm, a_hbm, table_hbm,
    out_ref,
    q_ref, g_ref, lw_ref, docs_ref, x_ref, a_ref, table,
    kv_buf, back_buf, doc_buf, bias, lw_t, w_buf, dq_ref, dv_ref,
    a_roll, z_in, f_ref,
    grad, low_buf, low_q_ref, mid_part, mid_buf, core_out, core_buf, stage, ry, rx, s2a, s2b, ry2, rx2,
    total, z_out, rz, z_sum, full,
    in_sem, q_sem, g_sem, kv_sem, doc_send, doc_recv, send_sem, recv_sem, back_recv,
    fz_send, fz_recv, fx_send, fx_recv, fc_send, fc_recv,
    low_send, low_recv, mid_send, mid_recv, core_send, core_recv,
    y_send, y_recv, x_send, x_recv, x2_send, x2_recv, y2_send, y2_recv,
    z_send, z_recv, f_send, f_recv,
):
    dp = lax.axis_index("dp")
    c = lax.axis_index("ctx")
    x, z = dp // NZ, dp % NZ
    y, core = c // 2, c % 2
    own = BLOCKS - 1

    def at(xx, zz, yy, cc):
        return (xx * NZ + zz, yy * 2 + cc)

    def ahead(value, step, size):
        return (value + step) % size

    def push(src, dst, send, recv, peer):
        return pltpu.make_async_remote_copy(
            src_ref=src, dst_ref=dst, send_sem=send, recv_sem=recv,
            device_id=peer, device_id_type=MESH)

    def cols_of(h, width):
        return pl.ds(pl.multiple_of(h * width, width), width)

    def kv_load(h, which):
        source = k_hbm if which == 0 else v_hbm
        return pltpu.make_async_copy(
            source.at[:, cols_of(h, HEAD)], kv_buf.at[h, own, which], kv_sem.at[h, which])

    def q_load(h):
        return pltpu.make_async_copy(
            q_hbm.at[:, cols_of(h, 1024)], q_ref.at[:, cols_of(h, 1024)], q_sem.at[h])

    def g_load(h):
        return pltpu.make_async_copy(
            g_hbm.at[:, cols_of(h, 1024)], g_ref.at[:, cols_of(h, 1024)], g_sem.at[h])

    small = [
        pltpu.make_async_copy(docs_hbm, docs_ref, in_sem.at[0]),
        pltpu.make_async_copy(a_hbm, a_ref, in_sem.at[1]),
        pltpu.make_async_copy(lw_hbm, lw_ref, in_sem.at[2]),
        pltpu.make_async_copy(table_hbm.at[c], table, in_sem.at[3]),
        pltpu.make_async_copy(x_hbm, x_ref, in_sem.at[4]),
    ]
    barrier = pltpu.get_barrier_semaphore()
    peers = [(dp, ahead(c, j, 8)) for j in range(1, 8)]
    peers += [at(ahead(x, d, NX), z, y, core) for d in range(1, NX)]
    peers += [at(x, ahead(z, d, NZ), y, core) for d in range(1, NZ)]
    for peer in peers:
        pl.semaphore_signal(barrier, inc=1, device_id=peer, device_id_type=MESH)
    small[0].start()
    small[1].start()

    def load_kv(h, carry):
        kv_load(h, 0).start()
        kv_load(h, 1).start()
        return carry

    lax.fori_loop(0, KV, load_kv, 0)
    small[2].start()
    small[3].start()

    def load_qg(h, carry):
        q_load(h).start()
        g_load(h).start()
        return carry

    lax.fori_loop(0, KV, load_qg, 0)
    small[4].start()

    for slot in range(own):
        @pl.when(c + slot < own)
        def _():
            doc_buf[slot] = jnp.full((8, ROWS), -1.0, F32)
            low_buf[slot] = jnp.zeros((RANK, ROWS), BF16)
            for h in range(KV):
                kv_buf[h, slot] = jnp.zeros((2, ROWS, HEAD), BF16)

        @pl.when(c + slot + 1 > 7)
        def _():
            mid_buf[slot] = jnp.zeros((RANK, ROWS), F32)

    small[0].wait()
    doc_buf[own] = jnp.broadcast_to(docs_ref[...].astype(F32), (8, ROWS))
    pl.semaphore_wait(barrier, len(peers))

    def doc_copy(j):
        return push(doc_buf.at[own], doc_buf.at[own - j], doc_send.at[j - 1],
                    doc_recv.at[own - j], (dp, c + j))

    def kv_copy(h, kind, source, target, peer):
        return push(kv_buf.at[h, source], kv_buf.at[h, target], send_sem.at[h, kind],
                    recv_sem.at[h, target], (dp, peer))

    def hop_own(h):
        return kv_copy(h, 0, 4, 2, c + 2)

    def pair_own(h):
        return kv_copy(h, 1, 4, 3, c + 1)

    def hop_relay(h):
        return kv_copy(h, 2, 2, 0, c + 2)

    def pair_near_up(h):
        return kv_copy(h, 3, 2, 1, c + 1)

    def pair_near_down(h):
        return kv_copy(h, 3, 2, 3, c - 1)

    def pair_far_down(h):
        return kv_copy(h, 4, 0, 1, c - 1)

    def back_own(h):
        return push(kv_buf.at[h, own], back_buf.at[h], send_sem.at[h, 5], back_recv.at[h],
                    (dp, ahead(c, 6, 8)))

    def back_relay(h):
        return push(back_buf.at[h], kv_buf.at[h, 0], send_sem.at[h, 6], recv_sem.at[h, 0],
                    (dp, ahead(c, 6, 8)))

    def is_back(h):
        return h % 2 == 1

    outer = jnp.logical_or(y == 0, y == 3)

    def send_own(h, carry):
        kv_load(h, 0).wait()
        kv_load(h, 1).wait()

        @pl.when(y < 3)
        def _():
            hop_own(h).start()

        @pl.when(core == 0)
        def _():
            pair_own(h).start()

        @pl.when(jnp.logical_and(is_back(h), y < 2))
        def _():
            back_own(h).start()
        return carry

    send_own(0, 0)
    for j in range(1, BLOCKS):
        @pl.when(c + j < 8)
        def _():
            doc_copy(j).start()
    send_own(1, 0)

    rank_rows = pl.ds(pl.multiple_of(core * HALF_ROWS, HALF_ROWS), HALF_ROWS)
    small[1].wait()
    a_roll[:, 512:WIN] = jnp.zeros((RANK, WIN - 512), F32)
    a_roll[:, 0:SHARD] = a_ref[...]
    offsets = (0, 96, 64, 32)
    for quarter in range(1, 4):
        @pl.when(z % 4 == quarter)
        def _():
            a_roll[...] = pltpu.roll(a_roll[...], offsets[quarter], axis=1)
    z_in[z] = a_roll[rank_rows, :].astype(BF16)

    span = (slice(0, 16), slice(16, 32))

    def fz_push(src, d, part):
        return push(z_in.at[src, span[part]], z_in.at[src, span[part]],
                    fz_send.at[part, d - 1], fz_recv.at[part, d - 1],
                    at(x, ahead(z, d, NZ), y, core))

    for part in range(2):
        for d in (4, 3, 5, 2, 6, 1, 7):
            fz_push(z, d, part).start()

    def section(xx):
        return pl.ds(pl.multiple_of(xx * XCOLS, HEAD), XCOLS)

    def half_section(xx, part):
        return pl.ds(pl.multiple_of(xx * XCOLS + part * HALF, HEAD), HALF)

    def f_rows(cc, part):
        return pl.ds(pl.multiple_of(cc * HALF_ROWS + part * 16, 16), 16)

    def fx_push(src, d, part):
        where = f_ref.at[f_rows(core, part), section(src)]
        return push(where, where, fx_send.at[part, d - 1], fx_recv.at[part, d - 1],
                    at(ahead(x, d, NX), z, y, core))

    def fc_push(cc, d, part):
        where = f_ref.at[f_rows(cc, part), section(ahead(x, NX - d, NX))]
        return push(where, where, fc_send.at[part, d], fc_recv.at[part, d],
                    at(x, z, y, 1 - core))

    def gather_block(part):
        for d in range(1, NZ):
            fz_push(ahead(z, NZ - d, NZ), d, part).wait_recv()
        for quad in range(2):
            w = [z_in[quad * 4 + i, span[part]] for i in range(4)]
            pieces = [
                w[0][:, 0:512], w[0][:, 512:640] + w[1][:, 0:128],
                w[1][:, 128:640], w[1][:, 640:768] + w[2][:, 0:128],
                w[2][:, 128:640], w[2][:, 640:768] + w[3][:, 0:128],
                w[3][:, 128:640],
            ]
            f_ref[f_rows(core, part), half_section(x, quad)] = jnp.concatenate(pieces, axis=1)
        for d in (2, 1, 3):
            fx_push(x, d, part).start()
        fc_push(core, 0, part).start()

    def gather_pair(part):
        for d in (1, 3, 2):
            fx_push(ahead(x, NX - d, NX), d, part).wait_recv()
            fc_push(core, d, part).start()

    def low_copy(j):
        return push(low_buf.at[own], low_buf.at[own - j], low_send.at[j - 1],
                    low_recv.at[own - j], (dp, c + j))

    def make_low():
        for part in range(2):
            for d in range(NX):
                fc_push(1 - core, d, part).wait_recv()
        small[4].wait()
        both = dot(jnp.concatenate([f_ref[:, D:2 * D], f_ref[:, 0:D]], axis=0), x_ref[...], NT)
        low_buf[own] = both[0:RANK].astype(BF16)
        for j in range(1, BLOCKS):
            @pl.when(c + j < 8)
            def _():
                low_copy(j).start()
        low_q_ref[...] = both[RANK:].astype(BF16)

    def relay_near(h):
        @pl.when(y >= 1)
        def _():
            hop_own(h).wait_recv()

            @pl.when(jnp.logical_and(jnp.logical_not(is_back(h)), y < 3))
            def _():
                hop_relay(h).start()

            @pl.when(core == 0)
            def _():
                pair_near_up(h).start()

            @pl.when(core == 1)
            def _():
                pair_near_down(h).start()

        @pl.when(jnp.logical_and(is_back(h), outer))
        def _():
            back_own(h).wait_recv()
            back_relay(h).start()

    def relay_far(h):
        @pl.when(y >= 2)
        def _():
            hop_relay(h).wait_recv()

            @pl.when(core == 1)
            def _():
                pair_far_down(h).start()

    def arrive(h):
        @pl.when(jnp.logical_or(core == 1, y >= 1))
        def _():
            pair_own(h).wait_recv()

        @pl.when(jnp.logical_or(y >= 2, jnp.logical_and(core == 1, y >= 1)))
        def _():
            pair_far_down(h).wait_recv()

    small[2].wait()
    lw_t[...] = jnp.broadcast_to(lw_ref[...].astype(F32), (ROWS, ROWS)).T

    relay_near(0)
    send_own(2, 0)
    relay_near(1)
    send_own(3, 0)
    for slot in range(own):
        @pl.when(c + slot >= own)
        def _():
            doc_copy(own - slot).wait_recv()
    doc_col = jnp.broadcast_to(doc_buf[own][0:1, :], (ROWS, ROWS)).T
    row_pos = lax.broadcasted_iota(jnp.int32, (ROWS, ROWS), 0)
    key_pos = lax.broadcasted_iota(jnp.int32, (ROWS, ROWS), 1)
    for slot in range(BLOCKS):
        allowed = jnp.broadcast_to(doc_buf[slot][0:1, :], (ROWS, ROWS)) == doc_col
        block = jnp.where(allowed, 0.0, NEG)
        if slot == 0:
            first_block = block
        elif slot == own:
            bias[:, 0:ROWS] = jnp.where(key_pos <= row_pos, block, first_block)
        else:
            bias[:, slot * ROWS:(slot + 1) * ROWS] = block
    small[3].wait()
    relay_near(2)
    send_own(4, 0)
    relay_far(0)

    scale = 1.0 / HEAD ** 0.5
    fold = scale * float(np.log2(np.e))
    part_heads = 4

    edge = own * ROWS

    def one_group(h, carry):
        lower = lax.broadcasted_iota(jnp.int32, (ROWS, ROWS), 1) <= lax.broadcasted_iota(
            jnp.int32, (ROWS, ROWS), 0)

        def fold_ends(a):
            return jnp.concatenate(
                [jnp.where(lower, a[:, edge:], a[:, 0:ROWS]), a[:, ROWS:edge]], axis=1)

        def unfold_ends(a):
            ends = a[:, 0:ROWS]
            return jnp.concatenate(
                [jnp.where(lower, 0.0, ends).astype(BF16), a[:, ROWS:].astype(BF16),
                 jnp.where(lower, ends, 0.0).astype(BF16)], axis=1)

        @pl.when(h + 3 < KV)
        def _():
            relay_near(h + 3)

        @pl.when(h + 5 < KV)
        def _():
            send_own(h + 5, 0)

        @pl.when(h + 1 < KV)
        def _():
            relay_far(h + 1)

        @pl.when(h == 0)
        def _():
            gather_block(0)

        @pl.when(h == 1)
        def _():
            gather_block(1)

        @pl.when(h == 4)
        def _():
            gather_pair(0)

        @pl.when(h == 6)
        def _():
            gather_pair(1)

        @pl.when(h == KV - 1)
        def _():
            make_low()

        q_load(h).wait()
        g_load(h).wait()
        arrive(h)
        keys = kv_buf[h, :, 0].reshape(WINDOW, HEAD)
        vals = kv_buf[h, :, 1].reshape(WINDOW, HEAD)

        def head_cols(i):
            return pl.ds(pl.multiple_of(h * GROUP * HEAD + i * HEAD, HEAD), HEAD)

        def front(part):
            heads = range(part * part_heads, (part + 1) * part_heads)
            queries = jnp.concatenate([q_ref[:, head_cols(i)] for i in heads], axis=0)
            weighted = jnp.concatenate(
                [(g_ref[:, head_cols(i)].astype(F32) * lw_t[...]).astype(BF16) for i in heads],
                axis=0)
            w_buf[part] = weighted
            return dot(queries, keys, NT), dot(weighted, vals, NT)

        parts = GROUP // part_heads
        ready = front(0)
        dv = None
        for part in range(parts):
            scores, dprobs = ready
            if part + 1 < parts:
                ready = front(part + 1)
            probs_b, dscores = [], []
            for t in range(part_heads):
                rows = slice(t * ROWS, (t + 1) * ROWS)
                masked = fold_ends(scores[rows]) + bias[...]
                top = jnp.max(masked, axis=1, keepdims=True)
                expo = jnp.exp2((masked - top) * fold)
                probs = expo * (1.0 / jnp.sum(expo, axis=1, keepdims=True))
                dp_rows = fold_ends(dprobs[rows])
                delta = jnp.sum(probs * dp_rows, axis=1, keepdims=True)
                probs_b.append(unfold_ends(probs))
                dscores.append(unfold_ends(probs * (dp_rows - delta)))
            dq = dot(jnp.concatenate(dscores, axis=0), keys, NN) * scale
            for t in range(part_heads):
                rot = dq[t * ROWS:(t + 1) * ROWS].astype(BF16).astype(F32)
                dq_ref[:, head_cols(part * part_heads + t)] = (
                    rot * table[0] + pltpu.roll(rot, HEAD // 2, axis=1) * table[1]).astype(BF16)
            more = dot(
                turn(w_buf[part]), jnp.concatenate(probs_b, axis=0), NN)
            dv = more if dv is None else dv + more
        dv_ref[cols_of(h, HEAD), :] = dv.astype(BF16)
        return carry

    lax.fori_loop(0, KV, one_group, 0)

    def mid_copy(j):
        return push(mid_part.at[own - j], mid_buf.at[j - 1], mid_send.at[j - 1],
                    mid_recv.at[j - 1], (dp, c - j))

    piece = dot(f_ref[:, BV:FACT], dv_ref[...], NN)
    for slot in range(BLOCKS):
        mid_part[slot] = piece[:, slot * ROWS:(slot + 1) * ROWS]
    for j in range(1, BLOCKS):
        @pl.when(c >= j)
        def _():
            mid_copy(j).start()

    def core_copy(part_x):
        return push(core_out.at[part_x], core_buf.at[part_x], core_send.at[part_x],
                    core_recv.at[part_x], at(x, z, y, 1 - core))

    def core_start(part_x):
        theirs = grad[:, pl.ds(
            pl.multiple_of(part_x * XCOLS + (1 - core) * HALF, HEAD), HALF)]
        core_out[part_x] = theirs.astype(BF16)
        core_copy(part_x).start()

    def y_rows(yy):
        return pl.ds(pl.multiple_of(yy * 16, 16), 16)

    def y_copy(d, part_x):
        yy = ahead(y, d, NY)
        return push(stage.at[part_x, y_rows(yy), 0:CUT], ry.at[d - 1, part_x],
                    y_send.at[d - 1, part_x], y_recv.at[d - 1, part_x], at(x, z, yy, core))

    def x_copy(d):
        xx = ahead(x, d, NX)
        return push(stage.at[xx, :, CUT:HALF], rx.at[d - 1],
                    x_send.at[d - 1], x_recv.at[d - 1], at(xx, z, y, core))

    def core_finish(part_x):
        core_copy(part_x).wait_recv()
        mine = grad[:, pl.ds(pl.multiple_of(part_x * XCOLS + core * HALF, HEAD), HALF)]
        stage[part_x] = (mine + core_buf[part_x].astype(F32)).astype(BF16)
        for d in (2, 1, 3):
            y_copy(d, part_x).start()
        for d in range(1, NX):
            @pl.when(ahead(x, d, NX) == part_x)
            def _():
                x_copy(d).start()

    for i in range(KV):
        grad[:, BQ + i * 1024:BQ + (i + 1) * 1024] = dot(
            low_q_ref[...], dq_ref[:, i * 1024:(i + 1) * 1024], NN)
    core_start(2 + core)
    mid_q = dot(f_ref[:, BQ:BV], dq_ref[...], NT).astype(BF16)
    for i in range(5):
        grad[:, i * 1024:(i + 1) * 1024] = dot(mid_q, x_ref[:, i * 1024:(i + 1) * 1024], NN)
    core_start(0)
    core_finish(3 - core)
    for slot in range(own):
        @pl.when(c + slot >= own)
        def _():
            low_copy(own - slot).wait_recv()
    low_window = jnp.concatenate([low_buf[s] for s in range(BLOCKS)], axis=1)
    grad[:, BV:FACT] = dot(low_window, dv_ref[...], NT)
    core_finish(0)
    mid_v = mid_part[own]
    for j in range(1, BLOCKS):
        @pl.when(c + j < 8)
        def _():
            mid_copy(j).wait_recv()
        mid_v = mid_v + mid_buf[j - 1]
    mid_v = mid_v.astype(BF16)
    for i in (4, 3, 2, 1, 0):
        grad[:, D + i * 1024:D + (i + 1) * 1024] = dot(
            mid_v, x_ref[:, i * 1024:(i + 1) * 1024], NN)
        if i == 4:
            core_start(3 - core)
    core_start(1)
    core_finish(2 + core)
    core_finish(1)

    def x2_copy(d):
        return push(s2a.at[d - 1], rx2.at[d - 1], x2_send.at[d - 1], x2_recv.at[d - 1],
                    at(ahead(x, d, NX), z, y, core))

    def y2_copy(d):
        return push(s2b.at[d - 1], ry2.at[d - 1], y2_send.at[d - 1], y2_recv.at[d - 1],
                    at(x, z, ahead(y, d, NY), core))

    for part_x in (3 - core, 0, 2 + core, 1):
        for d in range(1, NY):
            y_copy(d, part_x).wait_recv()
        value = stage[part_x, y_rows(y), 0:CUT].astype(F32)
        for e in range(NY - 1):
            value = value + ry[e, part_x].astype(F32)

        @pl.when(x == part_x)
        def _():
            total[:, 0:CUT] = value

        for d in range(1, NX):
            @pl.when(ahead(x, d, NX) == part_x)
            def _():
                s2a[d - 1] = value.astype(BF16)
                x2_copy(d).start()

    for d in range(1, NX):
        x_copy(d).wait_recv()
    for d in (1, 2, 3, 0):
        yy = ahead(y, d, NY)
        value = stage[x, y_rows(yy), CUT:HALF].astype(F32)
        for e in range(NX - 1):
            value = value + rx[e, y_rows(yy), :].astype(F32)
        if d:
            s2b[d - 1] = value.astype(BF16)
            y2_copy(d).start()
        else:
            total[:, CUT:HALF] = value
    for d in range(1, NX):
        x2_copy(d).wait_recv()
    value = total[:, 0:CUT]
    for e in range(NX - 1):
        value = value + rx2[e].astype(F32)
    total[:, 0:CUT] = value
    for d in range(1, NY):
        y2_copy(d).wait_recv()
    value = total[:, CUT:HALF]
    for e in range(NY - 1):
        value = value + ry2[e].astype(F32)
    total[:, CUT:HALF] = value
    z_out[...] = total[...].astype(BF16)

    starts = (0, 512, 1152, 1664)

    def z_copy(quarter, slot):
        return push(z_out.at[:, starts[quarter]:starts[quarter] + WIN], rz.at[slot],
                    z_send.at[quarter], z_recv.at[slot], at(x, core * 4 + quarter, y, core))

    for quarter in range(4):
        @pl.when(core * 4 + quarter != z)
        def _():
            z_copy(quarter, z).start()

    def full_copy(j):
        return push(full.at[y_rows(y)], full.at[y_rows(y)], f_send.at[j - 1],
                    f_recv.at[y], (dp, ahead(c, j, 8)))

    holder = z // 4

    @pl.when(core == holder)
    def _():
        for quarter in range(4):
            @pl.when(z % 4 == quarter)
            def _():
                z_sum[...] = total[:, starts[quarter]:starts[quarter] + WIN]
        value = z_sum[...]
        for s in range(1, NZ):
            slot = ahead(z, s, NZ)
            z_copy(0, slot).wait_recv()
            value = value + rz[slot].astype(F32)
        for quarter in range(4):
            @pl.when(z % 4 == quarter)
            def _():
                shift = quarter * SHARD - starts[quarter]
                moved = pltpu.roll(value, WIN - shift, axis=1) if shift else value
                full[y_rows(y), :] = moved[:, 0:640].astype(BF16)
        for j in range(1, 8):
            full_copy(j).start()

    def row_wait(yy):
        pltpu.make_async_remote_copy(
            src_ref=full.at[y_rows(yy)], dst_ref=full.at[y_rows(yy)], send_sem=f_send.at[0],
            recv_sem=f_recv.at[yy], device_id=(dp, ahead(c, 1, 8)),
            device_id_type=MESH).wait_recv()

    for d in range(1, NY):
        row_wait(ahead(y, d, NY))

    @pl.when(core != holder)
    def _():
        row_wait(y)

    out_ref[...] = full[...].astype(F32) * (ADAPTER_SCALE / (NX * NZ))

    for j in range(1, BLOCKS):
        @pl.when(c + j < 8)
        def _():
            doc_copy(j).wait_send()
            low_copy(j).wait_send()

        @pl.when(c >= j)
        def _():
            mid_copy(j).wait_send()

    def drain(h, carry):
        @pl.when(y < 3)
        def _():
            hop_own(h).wait_send()

        @pl.when(core == 0)
        def _():
            pair_own(h).wait_send()

        @pl.when(jnp.logical_and(is_back(h), y < 2))
        def _():
            back_own(h).wait_send()

        @pl.when(jnp.logical_and(is_back(h), outer))
        def _():
            back_relay(h).wait_send()

        @pl.when(y >= 1)
        def _():
            pair_near_up(h).wait_send()

        @pl.when(jnp.logical_and(jnp.logical_not(is_back(h)), jnp.logical_and(y >= 1, y < 3)))
        def _():
            hop_relay(h).wait_send()

        @pl.when(jnp.logical_and(y >= 2, core == 1))
        def _():
            pair_far_down(h).wait_send()
        return carry

    lax.fori_loop(0, KV, drain, 0)
    for part in range(2):
        for d in range(1, NZ):
            fz_push(z, d, part).wait_send()
        for d in range(1, NX):
            fx_push(x, d, part).wait_send()
        for d in range(NX):
            fc_push(core, d, part).wait_send()
    for part_x in range(NX):
        core_copy(part_x).wait_send()
        for d in range(1, NY):
            y_copy(d, part_x).wait_send()
    for d in range(1, NX):
        x_copy(d).wait_send()
        x2_copy(d).wait_send()
        y2_copy(d).wait_send()
    for quarter in range(4):
        @pl.when(core * 4 + quarter != z)
        def _():
            z_copy(quarter, z).wait_send()

    @pl.when(core == holder)
    def _():
        for j in range(1, 8):
            full_copy(j).wait_send()


def reduced_gradient(q, g, lw, docs, k, v, x, adapter):
    hbm = pl.BlockSpec(memory_space=pltpu.HBM)
    dma = pltpu.SemaphoreType.DMA
    mem = pltpu.VMEM
    return pl.pallas_call(
        kernel,
        out_shape=jax.ShapeDtypeStruct((RANK, 640), F32),
        in_specs=[hbm] * 9,
        out_specs=pl.BlockSpec(memory_space=pltpu.VMEM),
        scratch_shapes=[
            mem((ROWS, QW), BF16), mem((ROWS, QW), BF16),
            mem((1, ROWS), jnp.int32), mem((1, ROWS), jnp.int32),
            mem((ROWS, D), BF16), mem((RANK, SHARD), F32), mem((2, ROWS, HEAD), F32),
            mem((KV, BLOCKS, 2, ROWS, HEAD), BF16), mem((KV, 2, ROWS, HEAD), BF16),
            mem((BLOCKS, 8, ROWS), F32), mem((ROWS, WINDOW - ROWS), F32), mem((ROWS, ROWS), F32),
            mem((2, 4 * ROWS, HEAD), BF16),
            mem((ROWS, QW), BF16), mem((KV * HEAD, WINDOW), BF16),
            mem((RANK, WIN), F32), mem((NZ, HALF_ROWS, WIN), BF16), mem((RANK, FACT), BF16),
            mem((RANK, FACT), F32), mem((BLOCKS, RANK, ROWS), BF16), mem((RANK, ROWS), BF16),
            mem((BLOCKS, RANK, ROWS), F32), mem((BLOCKS - 1, RANK, ROWS), F32),
            mem((NX, RANK, HALF), BF16), mem((NX, RANK, HALF), BF16), mem((NX, RANK, HALF), BF16),
            mem((NY - 1, NX, 16, CUT), BF16), mem((NX - 1, RANK, REST), BF16),
            mem((NX - 1, 16, CUT), BF16), mem((NY - 1, 16, REST), BF16),
            mem((NY - 1, 16, REST), BF16), mem((NX - 1, 16, CUT), BF16),
            mem((16, HALF), F32), mem((16, HALF), BF16), mem((NZ, 16, WIN), BF16),
            mem((16, WIN), F32), mem((RANK, 640), BF16),
            dma((5,)), dma((KV,)), dma((KV,)), dma((KV, 2)), dma((4,)), dma((4,)),
            dma((KV, 7)), dma((KV, 4)), dma((KV,)),
            dma((2, 7)), dma((2, 7)), dma((2, 3)), dma((2, 3)), dma((2, 4)), dma((2, 4)),
            dma((4,)), dma((4,)), dma((4,)), dma((4,)), dma((4,)), dma((4,)),
            dma((3, 4)), dma((3, 4)), dma((3,)), dma((3,)),
            dma((3,)), dma((3,)), dma((3,)), dma((3,)),
            dma((4,)), dma((8,)), dma((7,)), dma((4,)),
        ],
        compiler_params=pltpu.CompilerParams(
            collective_id=0, has_side_effects=True, vmem_limit_bytes=60 * 1024 * 1024),
        cost_estimate=pl.CostEstimate(
            flops=8 * 64 * WINDOW * ROWS * HEAD + 4 * FACT * RANK * ROWS,
            bytes_accessed=10_000_000, transcendentals=64 * WINDOW * ROWS),
        name="layer_back",
    )(q, g, lw, docs, k, v, x, adapter, jnp.asarray(rope_tables()))


def per_device(
    normed_input, queries, keys, values, out_grad, loss_weight, doc_ids, adapter, moment1, moment2
):
    gradient = reduced_gradient(
        queries[0], out_grad[0], loss_weight, doc_ids, keys[0], values[0], normed_input[0],
        adapter)[:, 0:SHARD]
    new_m = BETA_ONE * moment1 + (1.0 - BETA_ONE) * gradient
    new_v = BETA_TWO * moment2 + (1.0 - BETA_TWO) * gradient * gradient
    corr_one = 1.0 - BETA_ONE ** STEP_COUNT
    corr_two = 1.0 - BETA_TWO ** STEP_COUNT
    return (new_m, new_v, new_m / corr_one / (jnp.sqrt(new_v / corr_two) + ADAM_EPS))


def solution(mesh):
    in_specs = (
        P("dp", "ctx", None),
        P("dp", "ctx", None),
        P("dp", "ctx", None),
        P("dp", "ctx", None),
        P("dp", "ctx", None),
        P("dp", "ctx"),
        P("dp", "ctx"),
        P(None, "dp"),
        P(None, "dp"),
        P(None, "dp"),
    )
    out_specs = (P(None, "dp"), P(None, "dp"), P(None, "dp"))
    return jax.shard_map(
        per_device, mesh=mesh, in_specs=in_specs, out_specs=out_specs, check_vma=False
    )
```

```python
import functools

import jax
import jax.numpy as jnp
import numpy as np
from jax import lax
from jax.experimental import pallas as pl
from jax.experimental.pallas import tpu as pltpu
from jax.sharding import PartitionSpec as P

HEAD = 128
GROUP = 8
KV = 8
D = 5120
RANK = 64
ROWS = 128
BLOCKS = 5
WINDOW = BLOCKS * ROWS
QW = KV * GROUP * HEAD
FACT = 2 * D + QW + KV * HEAD
BQ = 2 * D
BV = BQ + QW
NX, NZ, NY, NC = 4, 8, 4, 2
SHARD = FACT // (NX * NZ)
XCOLS = FACT // NX
HALF = XCOLS // 2
HALF_ROWS = RANK // 2
CUT = 1408
REST = HALF - CUT
WIN = 768

THETA = 1000000.0
ADAPTER_SCALE = 2.0
BETA_ONE = 0.9
BETA_TWO = 0.95
ADAM_EPS = 1e-08
STEP_COUNT = 10
NEG = -1e30
MESH = pl.DeviceIdType.MESH
NT = (((1,), (1,)), ((), ()))
NN = (((1,), (0,)), ((), ()))
F32 = jnp.float32
BF16 = jnp.bfloat16


def rope_tables():
    freq = THETA ** (-(np.arange(HEAD // 2, dtype=np.float64) * 2.0 / HEAD))
    angle = np.arange(NY * NC * ROWS, dtype=np.float64)[:, None] * freq[None, :]
    cosine, sine = np.cos(angle), np.sin(angle)
    both = np.stack(
        [np.concatenate([cosine, cosine], axis=1), np.concatenate([sine, -sine], axis=1)])
    return both.reshape(2, NY * NC, ROWS, HEAD).transpose(1, 0, 2, 3).astype(np.float32)


def dot(a, b, dims):
    return lax.dot_general(a, b, dims, preferred_element_type=F32)


def turn(a):
    return a.astype(F32).T.astype(BF16)


def kernel(
    q_hbm, g_hbm, lw_hbm, docs_hbm, k_hbm, v_hbm, x_hbm, a_hbm, table_hbm,
    out_ref,
    q_ref, g_ref, lw_ref, docs_ref, x_ref, a_ref, table,
    kv_buf, back_buf, doc_buf, bias, lw_t, w_buf, dq_ref, dv_ref,
    a_roll, z_in, f_ref,
    grad, low_buf, low_q_ref, mid_part, mid_buf, core_out, core_buf, stage, ry, rx, s2a, s2b, ry2, rx2,
    total, z_out, rz, z_sum, full,
    in_sem, q_sem, g_sem, kv_sem, doc_send, doc_recv, send_sem, recv_sem, back_recv,
    fz_send, fz_recv, fx_send, fx_recv, fc_send, fc_recv,
    low_send, low_recv, mid_send, mid_recv, core_send, core_recv,
    y_send, y_recv, x_send, x_recv, x2_send, x2_recv, y2_send, y2_recv,
    z_send, z_recv, f_send, f_recv,
):
    dp = lax.axis_index("dp")
    c = lax.axis_index("ctx")
    x, z = dp // NZ, dp % NZ
    y, core = c // 2, c % 2
    own = BLOCKS - 1

    def at(xx, zz, yy, cc):
        return (xx * NZ + zz, yy * 2 + cc)

    def ahead(value, step, size):
        return (value + step) % size

    def push(src, dst, send, recv, peer):
        return pltpu.make_async_remote_copy(
            src_ref=src, dst_ref=dst, send_sem=send, recv_sem=recv,
            device_id=peer, device_id_type=MESH)

    def cols_of(h, width):
        return pl.ds(pl.multiple_of(h * width, width), width)

    def kv_load(h, which):
        source = k_hbm if which == 0 else v_hbm
        return pltpu.make_async_copy(
            source.at[:, cols_of(h, HEAD)], kv_buf.at[h, own, which], kv_sem.at[h, which])

    def q_load(h):
        return pltpu.make_async_copy(
            q_hbm.at[:, cols_of(h, 1024)], q_ref.at[:, cols_of(h, 1024)], q_sem.at[h])

    def g_load(h):
        return pltpu.make_async_copy(
            g_hbm.at[:, cols_of(h, 1024)], g_ref.at[:, cols_of(h, 1024)], g_sem.at[h])

    small = [
        pltpu.make_async_copy(docs_hbm, docs_ref, in_sem.at[0]),
        pltpu.make_async_copy(a_hbm, a_ref, in_sem.at[1]),
        pltpu.make_async_copy(lw_hbm, lw_ref, in_sem.at[2]),
        pltpu.make_async_copy(table_hbm.at[c], table, in_sem.at[3]),
        pltpu.make_async_copy(x_hbm, x_ref, in_sem.at[4]),
    ]
    barrier = pltpu.get_barrier_semaphore()
    peers = [(dp, ahead(c, j, 8)) for j in range(1, 8)]
    peers += [at(ahead(x, d, NX), z, y, core) for d in range(1, NX)]
    peers += [at(x, ahead(z, d, NZ), y, core) for d in range(1, NZ)]
    for peer in peers:
        pl.semaphore_signal(barrier, inc=1, device_id=peer, device_id_type=MESH)
    small[0].start()
    small[1].start()

    def load_kv(h, carry):
        kv_load(h, 0).start()
        kv_load(h, 1).start()
        return carry

    lax.fori_loop(0, KV, load_kv, 0)
    small[2].start()
    small[3].start()

    def load_qg(h, carry):
        q_load(h).start()
        g_load(h).start()
        return carry

    lax.fori_loop(0, KV, load_qg, 0)
    small[4].start()

    for slot in range(own):
        @pl.when(c + slot < own)
        def _():
            doc_buf[slot] = jnp.full((8, ROWS), -1.0, F32)
            low_buf[slot] = jnp.zeros((RANK, ROWS), BF16)
            for h in range(KV):
                kv_buf[h, slot] = jnp.zeros((2, ROWS, HEAD), BF16)

        @pl.when(c + slot + 1 > 7)
        def _():
            mid_buf[slot] = jnp.zeros((RANK, ROWS), F32)

    small[0].wait()
    doc_buf[own] = jnp.broadcast_to(docs_ref[...].astype(F32), (8, ROWS))
    rank_rows = pl.ds(pl.multiple_of(core * HALF_ROWS, HALF_ROWS), HALF_ROWS)
    small[1].wait()
    a_roll[:, 512:WIN] = jnp.zeros((RANK, WIN - 512), F32)
    a_roll[:, 0:SHARD] = a_ref[...]
    offsets = (0, 96, 64, 32)
    for quarter in range(1, 4):
        @pl.when(z % 4 == quarter)
        def _():
            a_roll[...] = pltpu.roll(a_roll[...], offsets[quarter], axis=1)
    z_in[z] = a_roll[rank_rows, :].astype(BF16)

    small[2].wait()
    lw_t[...] = jnp.broadcast_to(lw_ref[...].astype(F32), (ROWS, ROWS)).T
    pl.semaphore_wait(barrier, len(peers))

    def doc_copy(j):
        return push(doc_buf.at[own], doc_buf.at[own - j], doc_send.at[j - 1],
                    doc_recv.at[own - j], (dp, c + j))

    def kv_copy(h, kind, source, target, peer):
        return push(kv_buf.at[h, source], kv_buf.at[h, target], send_sem.at[h, kind],
                    recv_sem.at[h, target], (dp, peer))

    def hop_own(h):
        return kv_copy(h, 0, 4, 2, c + 2)

    def pair_own(h):
        return kv_copy(h, 1, 4, 3, c + 1)

    def hop_relay(h):
        return kv_copy(h, 2, 2, 0, c + 2)

    def pair_near_up(h):
        return kv_copy(h, 3, 2, 1, c + 1)

    def pair_near_down(h):
        return kv_copy(h, 3, 2, 3, c - 1)

    def pair_far_down(h):
        return kv_copy(h, 4, 0, 1, c - 1)

    def back_own(h):
        return push(kv_buf.at[h, own], back_buf.at[h], send_sem.at[h, 5], back_recv.at[h],
                    (dp, ahead(c, 6, 8)))

    def back_relay(h):
        return push(back_buf.at[h], kv_buf.at[h, 0], send_sem.at[h, 6], recv_sem.at[h, 0],
                    (dp, ahead(c, 6, 8)))

    def is_back(h):
        return h % 2 == 1

    outer = jnp.logical_or(y == 0, y == 3)

    def send_own(h, carry):
        kv_load(h, 0).wait()
        kv_load(h, 1).wait()

        @pl.when(y < 3)
        def _():
            hop_own(h).start()

        @pl.when(core == 0)
        def _():
            pair_own(h).start()

        @pl.when(jnp.logical_and(is_back(h), y < 2))
        def _():
            back_own(h).start()
        return carry

    span = (slice(0, 16), slice(16, 32))

    def fz_push(src, d, part):
        return push(z_in.at[src, span[part]], z_in.at[src, span[part]],
                    fz_send.at[part, d - 1], fz_recv.at[part, d - 1],
                    at(x, ahead(z, d, NZ), y, core))

    for d in (4, 3, 5, 2, 6, 1, 7):
        fz_push(z, d, 0).start()
    send_own(0, 0)
    for j in range(1, BLOCKS):
        @pl.when(c + j < 8)
        def _():
            doc_copy(j).start()
    send_own(1, 0)
    for d in (4, 3, 5, 2, 6, 1, 7):
        fz_push(z, d, 1).start()


    def section(xx):
        return pl.ds(pl.multiple_of(xx * XCOLS, HEAD), XCOLS)

    def half_section(xx, part):
        return pl.ds(pl.multiple_of(xx * XCOLS + part * HALF, HEAD), HALF)

    def f_rows(cc, part):
        return pl.ds(pl.multiple_of(cc * HALF_ROWS + part * 16, 16), 16)

    def fx_push(src, d, part):
        where = f_ref.at[f_rows(core, part), section(src)]
        return push(where, where, fx_send.at[part, d - 1], fx_recv.at[part, d - 1],
                    at(ahead(x, d, NX), z, y, core))

    def fc_push(cc, d, part):
        where = f_ref.at[f_rows(cc, part), section(ahead(x, NX - d, NX))]
        return push(where, where, fc_send.at[part, d], fc_recv.at[part, d],
                    at(x, z, y, 1 - core))

    def gather_block(part):
        for d in range(1, NZ):
            fz_push(ahead(z, NZ - d, NZ), d, part).wait_recv()
        for quad in range(2):
            w = [z_in[quad * 4 + i, span[part]] for i in range(4)]
            pieces = [
                w[0][:, 0:512], w[0][:, 512:640] + w[1][:, 0:128],
                w[1][:, 128:640], w[1][:, 640:768] + w[2][:, 0:128],
                w[2][:, 128:640], w[2][:, 640:768] + w[3][:, 0:128],
                w[3][:, 128:640],
            ]
            f_ref[f_rows(core, part), half_section(x, quad)] = jnp.concatenate(pieces, axis=1)
        for d in (2, 1, 3):
            fx_push(x, d, part).start()
        fc_push(core, 0, part).start()

    def gather_pair(part):
        for d in (1, 3, 2):
            fx_push(ahead(x, NX - d, NX), d, part).wait_recv()
            fc_push(core, d, part).start()

    def low_copy(j):
        return push(low_buf.at[own], low_buf.at[own - j], low_send.at[j - 1],
                    low_recv.at[own - j], (dp, c + j))

    def make_low():
        for part in range(2):
            for d in range(NX):
                fc_push(1 - core, d, part).wait_recv()
        small[4].wait()
        both = dot(jnp.concatenate([f_ref[:, D:2 * D], f_ref[:, 0:D]], axis=0), x_ref[...], NT)
        low_buf[own] = both[0:RANK].astype(BF16)
        for j in range(1, BLOCKS):
            @pl.when(c + j < 8)
            def _():
                low_copy(j).start()
        low_q_ref[...] = both[RANK:].astype(BF16)

    def relay_near(h):
        @pl.when(y >= 1)
        def _():
            hop_own(h).wait_recv()

            @pl.when(jnp.logical_and(jnp.logical_not(is_back(h)), y < 3))
            def _():
                hop_relay(h).start()

            @pl.when(core == 0)
            def _():
                pair_near_up(h).start()

            @pl.when(core == 1)
            def _():
                pair_near_down(h).start()

        @pl.when(jnp.logical_and(is_back(h), outer))
        def _():
            back_own(h).wait_recv()
            back_relay(h).start()

    def relay_far(h):
        @pl.when(y >= 2)
        def _():
            hop_relay(h).wait_recv()

            @pl.when(core == 1)
            def _():
                pair_far_down(h).start()

    def arrive(h):
        @pl.when(jnp.logical_or(core == 1, y >= 1))
        def _():
            pair_own(h).wait_recv()

        @pl.when(jnp.logical_or(y >= 2, jnp.logical_and(core == 1, y >= 1)))
        def _():
            pair_far_down(h).wait_recv()


    relay_near(0)
    send_own(2, 0)
    relay_near(1)
    send_own(3, 0)
    for slot in range(own):
        @pl.when(c + slot >= own)
        def _():
            doc_copy(own - slot).wait_recv()
    doc_col = jnp.broadcast_to(doc_buf[own][0:1, :], (ROWS, ROWS)).T
    row_pos = lax.broadcasted_iota(jnp.int32, (ROWS, ROWS), 0)
    key_pos = lax.broadcasted_iota(jnp.int32, (ROWS, ROWS), 1)
    for slot in range(BLOCKS):
        allowed = jnp.broadcast_to(doc_buf[slot][0:1, :], (ROWS, ROWS)) == doc_col
        block = jnp.where(allowed, 0.0, NEG)
        if slot == 0:
            first_block = block
        elif slot == own:
            bias[:, 0:ROWS] = jnp.where(key_pos <= row_pos, block, first_block)
        else:
            bias[:, slot * ROWS:(slot + 1) * ROWS] = block
    small[3].wait()
    relay_near(2)
    send_own(4, 0)
    relay_far(0)

    scale = 1.0 / HEAD ** 0.5
    fold = scale * float(np.log2(np.e))
    part_heads = 4

    edge = own * ROWS

    def one_group(h, carry):
        lower = lax.broadcasted_iota(jnp.int32, (ROWS, ROWS), 1) <= lax.broadcasted_iota(
            jnp.int32, (ROWS, ROWS), 0)

        def fold_ends(a):
            return jnp.concatenate(
                [jnp.where(lower, a[:, edge:], a[:, 0:ROWS]), a[:, ROWS:edge]], axis=1)

        def unfold_ends(a):
            ends = a[:, 0:ROWS]
            return jnp.concatenate(
                [jnp.where(lower, 0.0, ends).astype(BF16), a[:, ROWS:].astype(BF16),
                 jnp.where(lower, ends, 0.0).astype(BF16)], axis=1)

        @pl.when(h + 3 < KV)
        def _():
            relay_near(h + 3)

        @pl.when(h + 5 < KV)
        def _():
            send_own(h + 5, 0)

        @pl.when(h + 1 < KV)
        def _():
            relay_far(h + 1)

        @pl.when(h == 0)
        def _():
            gather_block(0)

        @pl.when(h == 1)
        def _():
            gather_block(1)

        @pl.when(h == 4)
        def _():
            gather_pair(0)

        @pl.when(h == 6)
        def _():
            gather_pair(1)

        @pl.when(h == KV - 1)
        def _():
            make_low()

        q_load(h).wait()
        g_load(h).wait()
        arrive(h)
        keys = kv_buf[h, :, 0].reshape(WINDOW, HEAD)
        vals = kv_buf[h, :, 1].reshape(WINDOW, HEAD)

        def head_cols(i):
            return pl.ds(pl.multiple_of(h * GROUP * HEAD + i * HEAD, HEAD), HEAD)

        def front(part):
            heads = range(part * part_heads, (part + 1) * part_heads)
            queries = jnp.concatenate([q_ref[:, head_cols(i)] for i in heads], axis=0)
            weighted = jnp.concatenate(
                [(g_ref[:, head_cols(i)].astype(F32) * lw_t[...]).astype(BF16) for i in heads],
                axis=0)
            w_buf[part] = weighted
            return dot(queries, keys, NT), dot(weighted, vals, NT)

        parts = GROUP // part_heads
        ready = front(0)
        dv = None
        for part in range(parts):
            scores, dprobs = ready
            if part + 1 < parts:
                ready = front(part + 1)
            probs_b, dscores = [], []
            for t in range(part_heads):
                rows = slice(t * ROWS, (t + 1) * ROWS)
                masked = fold_ends(scores[rows]) + bias[...]
                top = jnp.max(masked, axis=1, keepdims=True)
                expo = jnp.exp2((masked - top) * fold)
                probs = expo * (1.0 / jnp.sum(expo, axis=1, keepdims=True))
                dp_rows = fold_ends(dprobs[rows])
                delta = jnp.sum(probs * dp_rows, axis=1, keepdims=True)
                probs_b.append(unfold_ends(probs))
                dscores.append(unfold_ends(probs * (dp_rows - delta)))
            dq = dot(jnp.concatenate(dscores, axis=0), keys, NN) * scale
            for t in range(part_heads):
                rot = dq[t * ROWS:(t + 1) * ROWS].astype(BF16).astype(F32)
                dq_ref[:, head_cols(part * part_heads + t)] = (
                    rot * table[0] + pltpu.roll(rot, HEAD // 2, axis=1) * table[1]).astype(BF16)
            more = dot(
                turn(w_buf[part]), jnp.concatenate(probs_b, axis=0), NN)
            dv = more if dv is None else dv + more
        dv_ref[cols_of(h, HEAD), :] = dv.astype(BF16)
        return carry

    lax.fori_loop(0, KV, one_group, 0)

    def mid_copy(j):
        return push(mid_part.at[own - j], mid_buf.at[j - 1], mid_send.at[j - 1],
                    mid_recv.at[j - 1], (dp, c - j))

    piece = dot(f_ref[:, BV:FACT], dv_ref[...], NN)
    for slot in range(BLOCKS):
        mid_part[slot] = piece[:, slot * ROWS:(slot + 1) * ROWS]
    for j in range(1, BLOCKS):
        @pl.when(c >= j)
        def _():
            mid_copy(j).start()

    def core_copy(part_x):
        return push(core_out.at[part_x], core_buf.at[part_x], core_send.at[part_x],
                    core_recv.at[part_x], at(x, z, y, 1 - core))

    def core_start(part_x):
        theirs = grad[:, pl.ds(
            pl.multiple_of(part_x * XCOLS + (1 - core) * HALF, HEAD), HALF)]
        core_out[part_x] = theirs.astype(BF16)
        core_copy(part_x).start()

    def y_rows(yy):
        return pl.ds(pl.multiple_of(yy * 16, 16), 16)

    def y_copy(d, part_x):
        yy = ahead(y, d, NY)
        return push(stage.at[part_x, y_rows(yy), 0:CUT], ry.at[d - 1, part_x],
                    y_send.at[d - 1, part_x], y_recv.at[d - 1, part_x], at(x, z, yy, core))

    def x_copy(d):
        xx = ahead(x, d, NX)
        return push(stage.at[xx, :, CUT:HALF], rx.at[d - 1],
                    x_send.at[d - 1], x_recv.at[d - 1], at(xx, z, y, core))

    def core_finish(part_x):
        core_copy(part_x).wait_recv()
        mine = grad[:, pl.ds(pl.multiple_of(part_x * XCOLS + core * HALF, HEAD), HALF)]
        stage[part_x] = (mine + core_buf[part_x].astype(F32)).astype(BF16)
        for d in (2, 1, 3):
            y_copy(d, part_x).start()
        for d in range(1, NX):
            @pl.when(ahead(x, d, NX) == part_x)
            def _():
                x_copy(d).start()

    for i in range(KV):
        grad[:, BQ + i * 1024:BQ + (i + 1) * 1024] = dot(
            low_q_ref[...], dq_ref[:, i * 1024:(i + 1) * 1024], NN)
    core_start(2 + core)
    mid_q = dot(f_ref[:, BQ:BV], dq_ref[...], NT).astype(BF16)
    for i in range(5):
        grad[:, i * 1024:(i + 1) * 1024] = dot(mid_q, x_ref[:, i * 1024:(i + 1) * 1024], NN)
    core_start(0)
    core_finish(3 - core)
    for slot in range(own):
        @pl.when(c + slot >= own)
        def _():
            low_copy(own - slot).wait_recv()
    low_window = jnp.concatenate([low_buf[s] for s in range(BLOCKS)], axis=1)
    grad[:, BV:FACT] = dot(low_window, dv_ref[...], NT)
    core_finish(0)
    mid_v = mid_part[own]
    for j in range(1, BLOCKS):
        @pl.when(c + j < 8)
        def _():
            mid_copy(j).wait_recv()
        mid_v = mid_v + mid_buf[j - 1]
    mid_v = mid_v.astype(BF16)
    for i in (4, 3, 2, 1, 0):
        grad[:, D + i * 1024:D + (i + 1) * 1024] = dot(
            mid_v, x_ref[:, i * 1024:(i + 1) * 1024], NN)
        if i == 4:
            core_start(3 - core)
    core_start(1)
    core_finish(2 + core)
    core_finish(1)

    def x2_copy(d):
        return push(s2a.at[d - 1], rx2.at[d - 1], x2_send.at[d - 1], x2_recv.at[d - 1],
                    at(ahead(x, d, NX), z, y, core))

    def y2_copy(d):
        return push(s2b.at[d - 1], ry2.at[d - 1], y2_send.at[d - 1], y2_recv.at[d - 1],
                    at(x, z, ahead(y, d, NY), core))

    for part_x in (3 - core, 0, 2 + core, 1):
        for d in range(1, NY):
            y_copy(d, part_x).wait_recv()
        value = stage[part_x, y_rows(y), 0:CUT].astype(F32)
        for e in range(NY - 1):
            value = value + ry[e, part_x].astype(F32)

        @pl.when(x == part_x)
        def _():
            total[:, 0:CUT] = value

        for d in range(1, NX):
            @pl.when(ahead(x, d, NX) == part_x)
            def _():
                s2a[d - 1] = value.astype(BF16)
                x2_copy(d).start()

    for d in range(1, NX):
        x_copy(d).wait_recv()
    for d in (1, 2, 3, 0):
        yy = ahead(y, d, NY)
        value = stage[x, y_rows(yy), CUT:HALF].astype(F32)
        for e in range(NX - 1):
            value = value + rx[e, y_rows(yy), :].astype(F32)
        if d:
            s2b[d - 1] = value.astype(BF16)
            y2_copy(d).start()
        else:
            total[:, CUT:HALF] = value
    for d in range(1, NX):
        x2_copy(d).wait_recv()
    value = total[:, 0:CUT]
    for e in range(NX - 1):
        value = value + rx2[e].astype(F32)
    total[:, 0:CUT] = value
    for d in range(1, NY):
        y2_copy(d).wait_recv()
    value = total[:, CUT:HALF]
    for e in range(NY - 1):
        value = value + ry2[e].astype(F32)
    total[:, CUT:HALF] = value
    z_out[...] = total[...].astype(BF16)

    starts = (0, 512, 1152, 1664)

    def z_copy(quarter, slot):
        return push(z_out.at[:, starts[quarter]:starts[quarter] + WIN], rz.at[slot],
                    z_send.at[quarter], z_recv.at[slot], at(x, core * 4 + quarter, y, core))

    for quarter in range(4):
        @pl.when(core * 4 + quarter != z)
        def _():
            z_copy(quarter, z).start()

    def full_copy(j):
        return push(full.at[y_rows(y)], full.at[y_rows(y)], f_send.at[j - 1],
                    f_recv.at[y], (dp, ahead(c, j, 8)))

    holder = z // 4

    @pl.when(core == holder)
    def _():
        for quarter in range(4):
            @pl.when(z % 4 == quarter)
            def _():
                z_sum[...] = total[:, starts[quarter]:starts[quarter] + WIN]
        value = z_sum[...]
        for s in range(1, NZ):
            slot = ahead(z, s, NZ)
            z_copy(0, slot).wait_recv()
            value = value + rz[slot].astype(F32)
        for quarter in range(4):
            @pl.when(z % 4 == quarter)
            def _():
                shift = quarter * SHARD - starts[quarter]
                moved = pltpu.roll(value, WIN - shift, axis=1) if shift else value
                full[y_rows(y), :] = moved[:, 0:640].astype(BF16)
        for j in range(1, 8):
            full_copy(j).start()

    def row_wait(yy):
        pltpu.make_async_remote_copy(
            src_ref=full.at[y_rows(yy)], dst_ref=full.at[y_rows(yy)], send_sem=f_send.at[0],
            recv_sem=f_recv.at[yy], device_id=(dp, ahead(c, 1, 8)),
            device_id_type=MESH).wait_recv()

    for d in range(1, NY):
        row_wait(ahead(y, d, NY))

    @pl.when(core != holder)
    def _():
        row_wait(y)

    out_ref[...] = full[...].astype(F32) * (ADAPTER_SCALE / (NX * NZ))

    for j in range(1, BLOCKS):
        @pl.when(c + j < 8)
        def _():
            doc_copy(j).wait_send()
            low_copy(j).wait_send()

        @pl.when(c >= j)
        def _():
            mid_copy(j).wait_send()

    def drain(h, carry):
        @pl.when(y < 3)
        def _():
            hop_own(h).wait_send()

        @pl.when(core == 0)
        def _():
            pair_own(h).wait_send()

        @pl.when(jnp.logical_and(is_back(h), y < 2))
        def _():
            back_own(h).wait_send()

        @pl.when(jnp.logical_and(is_back(h), outer))
        def _():
            back_relay(h).wait_send()

        @pl.when(y >= 1)
        def _():
            pair_near_up(h).wait_send()

        @pl.when(jnp.logical_and(jnp.logical_not(is_back(h)), jnp.logical_and(y >= 1, y < 3)))
        def _():
            hop_relay(h).wait_send()

        @pl.when(jnp.logical_and(y >= 2, core == 1))
        def _():
            pair_far_down(h).wait_send()
        return carry

    lax.fori_loop(0, KV, drain, 0)
    for part in range(2):
        for d in range(1, NZ):
            fz_push(z, d, part).wait_send()
        for d in range(1, NX):
            fx_push(x, d, part).wait_send()
        for d in range(NX):
            fc_push(core, d, part).wait_send()
    for part_x in range(NX):
        core_copy(part_x).wait_send()
        for d in range(1, NY):
            y_copy(d, part_x).wait_send()
    for d in range(1, NX):
        x_copy(d).wait_send()
        x2_copy(d).wait_send()
        y2_copy(d).wait_send()
    for quarter in range(4):
        @pl.when(core * 4 + quarter != z)
        def _():
            z_copy(quarter, z).wait_send()

    @pl.when(core == holder)
    def _():
        for j in range(1, 8):
            full_copy(j).wait_send()


def reduced_gradient(q, g, lw, docs, k, v, x, adapter):
    hbm = pl.BlockSpec(memory_space=pltpu.HBM)
    dma = pltpu.SemaphoreType.DMA
    mem = pltpu.VMEM
    return pl.pallas_call(
        kernel,
        out_shape=jax.ShapeDtypeStruct((RANK, 640), F32),
        in_specs=[hbm] * 9,
        out_specs=pl.BlockSpec(memory_space=pltpu.VMEM),
        scratch_shapes=[
            mem((ROWS, QW), BF16), mem((ROWS, QW), BF16),
            mem((1, ROWS), jnp.int32), mem((1, ROWS), jnp.int32),
            mem((ROWS, D), BF16), mem((RANK, SHARD), F32), mem((2, ROWS, HEAD), F32),
            mem((KV, BLOCKS, 2, ROWS, HEAD), BF16), mem((KV, 2, ROWS, HEAD), BF16),
            mem((BLOCKS, 8, ROWS), F32), mem((ROWS, WINDOW - ROWS), F32), mem((ROWS, ROWS), F32),
            mem((2, 4 * ROWS, HEAD), BF16),
            mem((ROWS, QW), BF16), mem((KV * HEAD, WINDOW), BF16),
            mem((RANK, WIN), F32), mem((NZ, HALF_ROWS, WIN), BF16), mem((RANK, FACT), BF16),
            mem((RANK, FACT), F32), mem((BLOCKS, RANK, ROWS), BF16), mem((RANK, ROWS), BF16),
            mem((BLOCKS, RANK, ROWS), F32), mem((BLOCKS - 1, RANK, ROWS), F32),
            mem((NX, RANK, HALF), BF16), mem((NX, RANK, HALF), BF16), mem((NX, RANK, HALF), BF16),
            mem((NY - 1, NX, 16, CUT), BF16), mem((NX - 1, RANK, REST), BF16),
            mem((NX - 1, 16, CUT), BF16), mem((NY - 1, 16, REST), BF16),
            mem((NY - 1, 16, REST), BF16), mem((NX - 1, 16, CUT), BF16),
            mem((16, HALF), F32), mem((16, HALF), BF16), mem((NZ, 16, WIN), BF16),
            mem((16, WIN), F32), mem((RANK, 640), BF16),
            dma((5,)), dma((KV,)), dma((KV,)), dma((KV, 2)), dma((4,)), dma((4,)),
            dma((KV, 7)), dma((KV, 4)), dma((KV,)),
            dma((2, 7)), dma((2, 7)), dma((2, 3)), dma((2, 3)), dma((2, 4)), dma((2, 4)),
            dma((4,)), dma((4,)), dma((4,)), dma((4,)), dma((4,)), dma((4,)),
            dma((3, 4)), dma((3, 4)), dma((3,)), dma((3,)),
            dma((3,)), dma((3,)), dma((3,)), dma((3,)),
            dma((4,)), dma((8,)), dma((7,)), dma((4,)),
        ],
        compiler_params=pltpu.CompilerParams(
            collective_id=0, has_side_effects=True, vmem_limit_bytes=60 * 1024 * 1024),
        cost_estimate=pl.CostEstimate(
            flops=8 * 64 * WINDOW * ROWS * HEAD + 4 * FACT * RANK * ROWS,
            bytes_accessed=10_000_000, transcendentals=64 * WINDOW * ROWS),
        name="layer_back",
    )(q, g, lw, docs, k, v, x, adapter, jnp.asarray(rope_tables()))


def per_device(
    normed_input, queries, keys, values, out_grad, loss_weight, doc_ids, adapter, moment1, moment2
):
    gradient = reduced_gradient(
        queries[0], out_grad[0], loss_weight, doc_ids, keys[0], values[0], normed_input[0],
        adapter)[:, 0:SHARD]
    new_m = BETA_ONE * moment1 + (1.0 - BETA_ONE) * gradient
    new_v = BETA_TWO * moment2 + (1.0 - BETA_TWO) * gradient * gradient
    corr_one = 1.0 - BETA_ONE ** STEP_COUNT
    corr_two = 1.0 - BETA_TWO ** STEP_COUNT
    return (new_m, new_v, new_m / corr_one / (jnp.sqrt(new_v / corr_two) + ADAM_EPS))


def solution(mesh):
    in_specs = (
        P("dp", "ctx", None),
        P("dp", "ctx", None),
        P("dp", "ctx", None),
        P("dp", "ctx", None),
        P("dp", "ctx", None),
        P("dp", "ctx"),
        P("dp", "ctx"),
        P(None, "dp"),
        P(None, "dp"),
        P(None, "dp"),
    )
    out_specs = (P(None, "dp"), P(None, "dp"), P(None, "dp"))
    return jax.shard_map(
        per_device, mesh=mesh, in_specs=in_specs, out_specs=out_specs, check_vma=False
    )
```
